32 devices in a mesh: sec: 4 (over x, core), tile: 8 (over z, y).
Axes of the slice: x: 2, y: 2, z: 4, core: 2. Of those that a mesh axis runs over, the one named last changes fastest.
Arguments:
- intersection_faces: bfloat16 [256, 1, 128, 128], P(('sec', 'tile')), may hold values from -6 to 6
- destination: int32 [256, 1], P(('sec', 'tile')), may hold values from 0 to 7; in each aligned block of 8 rows (0 to 7, 8 to 15, ...) at most 2 rows name the same one
- partner: int32 [256], P(('sec', 'tile')), may hold values from 0 to 7
- face_peaks: int32 [256, 2, 8], P(('sec', 'tile')), may hold values from 0 to 127
- coarse: bfloat16 [64, 256, 256], P(('sec', 'tile')), may hold values from -6 to 6
- coarse_peaks: int32 [256, 2, 8], P(('sec', 'tile')), may hold values from 0 to 255
- upper_faces: bfloat16 [64, 1, 128, 128], P(('sec', 'tile')), may hold values from -6 to 6
- lower_faces: bfloat16 [64, 1, 128, 128], P(('sec', 'tile')), may hold values from -6 to 6
- section_peaks: int32 [64, 2, 8], P(('sec', 'tile')), may hold values from 0 to 127
Outputs:
- fine_scores: float32 [256, 1, 8], P(('sec', 'tile'))
- coarse_scores: float32 [256, 8], P(('sec', 'tile'))
- section_scores: float32 [64, 1, 8], P(('sec', 'tile'))
The draws below stay inside these ranges and needn't reach their ends.
Inputs may be any that keep to these rules, and one draw needn't show every extreme that they name: `destination`: in each aligned block of 8 rows (the faces of one device) no value appears more than 2 times.
All inputs are finite; a program needn't handle non-finite values.
Results may differ from the reference program's by a relative error of at most 0.012.
The reference program's roundings to bfloat16 on the way count: a program that leaves them out, or rounds other values in their place, can miss the bound.
Values may be sent and summed in bfloat16 or wider, within the bound.
A program may use at most 64 MiB of HBM per device.

```python
import math
import jax
import jax.numpy as jnp
import numpy as np
from jax import lax

WIN = 128
CS = 256
PEAKS = 8
FACES_TILE = 4
WINF = 1
TILE_DEV = 2
FACE_DEV = 8
CAP = 2
FACES = 256
TILES = 64
N_TILE = 8


def with_ends(drawn, rng, low, largest):
    spot = [jax.random.randint(jax.random.fold_in(rng, axis), (), 0, length) for axis, length in enumerate(drawn.shape)]
    longest = drawn.shape.index(max(drawn.shape))
    next_to = spot[:longest] + [(spot[longest] + 1) % drawn.shape[longest]] + spot[longest + 1:]
    return drawn.at[tuple(spot)].set(low).at[tuple(next_to)].set(largest)


def block_levels(key, shape, pieces, low, high):
    def one(position, blocks):
        heights = jax.random.uniform(jax.random.fold_in(jax.random.fold_in(key, 6), position), (blocks,), jnp.float32, low / len(pieces), high / len(pieces))
        return jnp.repeat(jnp.exp(heights), shape[position] // blocks).reshape((-1,) + (1,) * (len(shape) - position - 1))

    level = one(*pieces[0])
    for cut in pieces[1:]:
        level = level * one(*cut)
    return level


def assign_block(own_key, own, number, rows, number_of, top, limit, skew):
    ranking = jax.random.permutation(own_key, number_of)
    heavy_load, usual = shares(number_of, rows * top, limit, skew, True), shares(number_of, rows * top, limit, skew, False)
    places = jnp.arange(number_of)

    def named(lengths, offset_by):
        used = int((lengths > 0).sum())
        fixed = max(1, used // 4)
        shifted = fixed + (places - fixed + offset_by * (used - fixed)) % max(1, number_of - fixed)
        return jnp.zeros((number_of,), jnp.int32).at[ranking[jnp.where(places < fixed, places, shifted)]].set(jnp.asarray(lengths, jnp.int32))

    lengths = jnp.where(number % 4 == 0, named(heavy_load, number // 4), named(usual, number - number // 4 - 1))
    mixed = jax.random.permutation(jax.random.fold_in(own, 3), number_of)
    donor, receiver = mixed[0:number_of // 2 * 2:2], mixed[1:number_of // 2 * 2:2]
    margin = jnp.minimum(lengths[donor] - 1, limit - lengths[receiver]) // 2
    margin = jnp.where((donor == ranking[0]) | (receiver == ranking[0]) | (lengths[receiver] == 0), 0, jnp.maximum(margin, 0))
    shifted = jax.random.randint(jax.random.fold_in(own, 4), (number_of // 2,), 0, 1 << 20) % (margin + 1)
    lengths = lengths.at[donor].add(-shifted).at[receiver].add(shifted)
    members = jnp.searchsorted(jnp.cumsum(lengths), jnp.arange(rows * top), side="right").astype(jnp.int32)
    listing = members.reshape(top, rows).T
    listing = listing[jax.random.permutation(jax.random.fold_in(own, 1), rows)]
    offset_by = jax.random.randint(jax.random.fold_in(own, 2), (rows, 1), 0, top)
    return jnp.take_along_axis(listing, (jnp.arange(top)[None, :] + offset_by) % top, axis=1)


def shares(amount, total, bound, slope, full):
    weights = [(1 << 20) // math.isqrt(grade ** slope) + 1 for grade in range(1, amount + 1)]
    largest = bound if full else min(bound, max(-(-total // amount), total * weights[0] // sum(weights)))
    least = 1 if total - largest >= amount - 1 else 0
    given, surplus = [largest] + [least] * (amount - 1), total - largest - least * (amount - 1)
    while surplus > 0:
        movable = [i for i in range(1, amount) if given[i] < largest] or [i for i in range(1, amount) if given[i] < bound]
        whole, budget = sum([weights[i] for i in movable]), surplus
        for i in movable:
            addition = min(bound - given[i], max(1, budget * weights[i] // whole), surplus)
            given[i] = given[i] + addition
            surplus = surplus - addition
    return np.array(given)


def bell_draw(own_key, shape, width, most, shards=(), held_as=jnp.bfloat16):
    result = jax.random.normal(own_key, shape, jnp.float32) * width
    if len(shards) > 0:
        result = block_levels(own_key, shape, shards, -0.22, 0.18) * result
    return jnp.clip(result, min=-most, max=most).astype(held_as)


def setup_inputs(seed: int = 0) -> dict:
    streams_of = jax.random.split(jax.random.key(seed), 10)
    intersection_faces = bell_draw(streams_of[0], (FACES, WINF, WIN, WIN), 1.0, 6.0, ((0, 32),))
    destination_keys = jax.random.split(jax.random.fold_in(streams_of[1], 1), FACES // FACE_DEV)
    destination_turns = jax.random.permutation(jax.random.fold_in(streams_of[1], 3), FACES // FACE_DEV)
    destination = jax.vmap(lambda own, number: assign_block(jax.random.fold_in(streams_of[1], 2), own, number, FACE_DEV, N_TILE, 1, CAP, 2))(destination_keys, destination_turns).reshape((FACES, 1))
    partner = with_ends(jax.random.randint(streams_of[2], (FACES,), 0, FACE_DEV), jax.random.fold_in(streams_of[2], 1), 0, FACE_DEV - 1).astype(jnp.int32)
    face_peaks = with_ends(jax.random.randint(streams_of[3], (FACES, 2, PEAKS), 0, WIN), jax.random.fold_in(streams_of[3], 1), 0, WIN - 1).astype(jnp.int32)
    coarse = bell_draw(streams_of[4], (TILES, CS, CS), 1.0, 6.0, ((0, 32),))
    coarse_peaks = with_ends(jax.random.randint(streams_of[5], (FACES, 2, PEAKS), 0, CS), jax.random.fold_in(streams_of[5], 1), 0, CS - 1).astype(jnp.int32)
    upper_faces = bell_draw(streams_of[6], (TILES, WINF, WIN, WIN), 1.0, 6.0, ((0, 32),))
    lower_faces = bell_draw(streams_of[7], (TILES, WINF, WIN, WIN), 1.0, 6.0, ((0, 32),))
    section_peaks = with_ends(jax.random.randint(streams_of[8], (TILES, 2, PEAKS), 0, WIN), jax.random.fold_in(streams_of[8], 1), 0, WIN - 1).astype(jnp.int32)
    return {"intersection_faces": intersection_faces, "destination": destination, "partner": partner, "face_peaks": face_peaks, "coarse": coarse, "coarse_peaks": coarse_peaks, "upper_faces": upper_faces, "lower_faces": lower_faces, "section_peaks": section_peaks}


TWO_PI = 6.283185307179586

def window_weights(extent):
    positions = jnp.arange(extent, dtype=jnp.float32)
    return 0.5 - 0.5 * jnp.cos((positions + 0.5) * (TWO_PI / extent))

def dft_tables(extent):
    indices = jnp.arange(extent, dtype=jnp.int32)
    angles = (indices[:, None] * indices[None, :] % extent).astype(jnp.float32) * (TWO_PI / extent)
    return (jnp.cos(angles).astype(jnp.bfloat16), jnp.sin(angles).astype(jnp.bfloat16))

def spectrum(images):
    extent = images.shape[-1]
    weights = window_weights(extent)
    shaped = (images.astype(jnp.float32) * weights[:, None] * weights[None, :]).astype(jnp.bfloat16)
    cosine, sine_table = dft_tables(extent)
    segment_tables = jnp.stack([cosine, sine_table])
    segment_one = jnp.einsum('jkx,...xy->...jky', segment_tables.astype(jnp.float32), shaped.astype(jnp.float32), precision=lax.Precision.HIGHEST).astype(jnp.bfloat16)
    second_tables = jnp.stack([jnp.concatenate([cosine, sine_table], axis=1), jnp.concatenate([-sine_table, cosine], axis=1)])
    segment_two = jnp.einsum('...jky,jyl->...kl', segment_one.astype(jnp.float32), second_tables.astype(jnp.float32), precision=lax.Precision.HIGHEST)
    return (segment_two[..., :extent], -segment_two[..., extent:])

def correlate(own_spec, other_spec, peak_marks):
    own_real, own_imag = own_spec
    other_real, other_imag = other_spec
    cross_real = own_real * other_real + own_imag * other_imag
    cross_imag = own_imag * other_real - own_real * other_imag
    magnitude = jnp.sqrt(cross_real * cross_real + cross_imag * cross_imag)
    floor_value = 0.05 * lax.optimization_barrier(jnp.mean(magnitude, axis=(-2, -1), keepdims=True)) + 1e-06
    divisor = jnp.maximum(magnitude, floor_value)
    unit_real = cross_real / divisor
    unit_imag = cross_imag / divisor
    extent = own_real.shape[-1]
    indices = jnp.arange(extent, dtype=jnp.int32)
    row_angles = (peak_marks[..., 0, :, None] * indices % extent).astype(jnp.float32) * (TWO_PI / extent)
    col_angles = (peak_marks[..., 1, :, None] * indices % extent).astype(jnp.float32) * (TWO_PI / extent)
    row_cos = jnp.cos(row_angles)
    row_sin = jnp.sin(row_angles)
    high = lax.Precision.HIGHEST
    first_real = jnp.einsum('...pk,...kl->...pl', row_cos, unit_real, precision=high) - jnp.einsum('...pk,...kl->...pl', row_sin, unit_imag, precision=high)
    first_imag = jnp.einsum('...pk,...kl->...pl', row_cos, unit_imag, precision=high) + jnp.einsum('...pk,...kl->...pl', row_sin, unit_real, precision=high)
    return lax.optimization_barrier(jnp.sum(first_real * jnp.cos(col_angles) - first_imag * jnp.sin(col_angles), axis=-1)) / extent

def reference(intersection_faces, destination, partner, face_peaks, coarse, coarse_peaks, upper_faces, lower_faces, section_peaks):
    face_count = intersection_faces.shape[0]
    face_index = jnp.arange(face_count, dtype=jnp.int32)
    device = face_index // FACE_DEV
    section = device // N_TILE
    pair_device = section * N_TILE + destination[:, 0]
    partner_face = pair_device * FACE_DEV + partner
    own_tile = face_index // FACES_TILE
    partner_tile = pair_device * TILE_DEV + partner // FACES_TILE
    windows = intersection_faces.shape[1]

    def fine_one(which):
        own_spec = spectrum(intersection_faces[which])
        other_spec = spectrum(intersection_faces[partner_face[which]])
        peak_marks = jnp.broadcast_to(face_peaks[which][None], (windows, 2, PEAKS))
        return correlate(own_spec, other_spec, peak_marks)
    fine_scores = lax.map(fine_one, face_index, batch_size=64)
    coarse_real, coarse_imag = lax.map(spectrum, coarse, batch_size=16)

    def coarse_one(which):
        own_spec = (coarse_real[own_tile[which]], coarse_imag[own_tile[which]])
        other_spec = (coarse_real[partner_tile[which]], coarse_imag[partner_tile[which]])
        return correlate(own_spec, other_spec, coarse_peaks[which])
    coarse_scores = lax.map(coarse_one, face_index, batch_size=64)
    tile_count = upper_faces.shape[0]
    tile_index = jnp.arange(tile_count, dtype=jnp.int32)
    per_section = TILE_DEV * N_TILE
    below_index = jnp.maximum(tile_index - per_section, 0)
    has_below = tile_index >= per_section

    def section_one(which):
        lower_in = jnp.where(has_below[which], lower_faces[below_index[which]], jnp.zeros_like(lower_faces[0]))
        peak_marks = jnp.broadcast_to(section_peaks[which][None], (windows, 2, PEAKS))
        return correlate(spectrum(upper_faces[which]), spectrum(lower_in), peak_marks)
    section_scores = lax.map(section_one, tile_index, batch_size=64)
    return (fine_scores, coarse_scores, section_scores)
```

```python
import functools

import jax
import jax.numpy as jnp
import ml_dtypes
import numpy as np
from jax import lax
from jax.experimental import pallas as pl
from jax.experimental.pallas import tpu as pltpu
from jax.sharding import PartitionSpec as P

TWO_PI = 6.283185307179586
LANES = 128
MESH = pl.DeviceIdType.MESH


def from_behind(value, axis, steps):
    count = lax.axis_size(axis)
    first, last = (max(0, -steps), min(count, count - steps))
    return lax.ppermute(value, axis, [(source, source + steps) for source in range(first, last)])


def window_weights(extent):
    positions = jnp.arange(extent, dtype=jnp.float32)
    return 0.5 - 0.5 * jnp.cos((positions + 0.5) * (TWO_PI / extent))


def dft_tables(extent):
    indices = jnp.arange(extent, dtype=jnp.int32)
    angles = (indices[:, None] * indices[None, :] % extent).astype(jnp.float32) * (TWO_PI / extent)
    return (jnp.cos(angles).astype(jnp.bfloat16), jnp.sin(angles).astype(jnp.bfloat16))


def spectrum(images):
    extent = images.shape[-1]
    weights = window_weights(extent)
    shaped = (images.astype(jnp.float32) * weights[:, None] * weights[None, :]).astype(jnp.bfloat16)
    cosine, sine_table = dft_tables(extent)
    segment_tables = jnp.stack([cosine, sine_table])
    segment_one = jnp.einsum(
        "jkx,...xy->...jky", segment_tables, shaped, preferred_element_type=jnp.float32
    ).astype(jnp.bfloat16)
    second_tables = jnp.stack(
        [
            jnp.concatenate([cosine, sine_table], axis=1),
            jnp.concatenate([-sine_table, cosine], axis=1),
        ]
    )
    segment_two = jnp.einsum(
        "...jky,jyl->...kl", segment_one, second_tables, preferred_element_type=jnp.float32
    )
    return (segment_two[..., :extent], -segment_two[..., extent:])


def correlate(own_spec, other_spec, peak_marks):
    own_real, own_imag = own_spec
    other_real, other_imag = other_spec
    cross_real = own_real * other_real + own_imag * other_imag
    cross_imag = own_imag * other_real - own_real * other_imag
    magnitude = jnp.sqrt(cross_real * cross_real + cross_imag * cross_imag)
    floor_value = 0.05 * jnp.mean(magnitude, axis=(-2, -1), keepdims=True) + 1e-06
    divisor = jnp.maximum(magnitude, floor_value)
    unit_real = cross_real / divisor
    unit_imag = cross_imag / divisor
    extent = own_real.shape[-1]
    indices = jnp.arange(extent, dtype=jnp.int32)
    row_angles = (peak_marks[..., 0, :, None] * indices % extent).astype(jnp.float32) * (
        TWO_PI / extent
    )
    col_angles = (peak_marks[..., 1, :, None] * indices % extent).astype(jnp.float32) * (
        TWO_PI / extent
    )
    row_cos = jnp.cos(row_angles)
    row_sin = jnp.sin(row_angles)
    high = lax.Precision.HIGHEST
    first_real = jnp.einsum("...pk,...kl->...pl", row_cos, unit_real, precision=high) - jnp.einsum(
        "...pk,...kl->...pl", row_sin, unit_imag, precision=high
    )
    first_imag = jnp.einsum("...pk,...kl->...pl", row_cos, unit_imag, precision=high) + jnp.einsum(
        "...pk,...kl->...pl", row_sin, unit_real, precision=high
    )
    return (
        jnp.sum(first_real * jnp.cos(col_angles) - first_imag * jnp.sin(col_angles), axis=-1)
        / extent
    )


def body(
    intersection_faces,
    destination,
    partner,
    face_peaks,
    coarse,
    coarse_peaks,
    upper_faces,
    lower_faces,
    section_peaks,
):
    face_dev = intersection_faces.shape[0]
    tile_dev = coarse.shape[0]
    per_tile = face_dev // tile_dev
    windows = intersection_faces.shape[1]
    peak_count = face_peaks.shape[2]
    tile_count = lax.axis_size("tile")
    capacity = max(2, (face_dev + tile_count - 1) // tile_count)
    slot_count = tile_count * capacity
    target = destination[:, 0]
    face_order = jnp.arange(face_dev, dtype=jnp.int32)
    earlier = (target[None, :] == target[:, None]) & (face_order[None, :] < face_order[:, None])
    position = jnp.sum(earlier.astype(jnp.int32), axis=1)
    slot_of = target * capacity + position
    slot_match = slot_of[None, :] == jnp.arange(slot_count, dtype=jnp.int32)[:, None]
    filled = jnp.any(slot_match, axis=1)
    source = jnp.sum(jnp.where(slot_match, face_order[None, :], 0), axis=1)
    requests = jnp.where(filled, partner[source] + 1, 0).reshape(tile_count, capacity)
    own_real, own_imag = spectrum(intersection_faces)
    parcel = jnp.einsum(
        "sf,fwxy->swxy", slot_match.astype(jnp.bfloat16), intersection_faces,
        preferred_element_type=jnp.float32,
    ).astype(jnp.bfloat16)
    parcel = parcel.reshape((tile_count, capacity) + intersection_faces.shape[1:])
    peak_marks = jnp.sum(
        jnp.where(slot_match[:, :, None, None], face_peaks[None], 0), axis=1
    ).reshape((tile_count, capacity) + face_peaks.shape[1:])
    got_faces, got_marks, wanted_ids = (
        lax.all_to_all(parcel, "tile", split_axis=0, concat_axis=0, tiled=True),
        lax.all_to_all(peak_marks, "tile", split_axis=0, concat_axis=0, tiled=True),
        lax.all_to_all(requests, "tile", split_axis=0, concat_axis=0, tiled=True),
    )

    def one_slot(packed):
        face_in, mark_in, wanted = packed
        chosen_slot = jnp.maximum(wanted - 1, 0)
        own_part = (own_real[chosen_slot], own_imag[chosen_slot])
        marks_all = mark_in[None]
        scores = correlate(spectrum(face_in), own_part, marks_all)
        return jnp.where(wanted > 0, scores, jnp.zeros_like(scores))

    slot_scores = lax.map(
        one_slot,
        (
            got_faces.reshape((slot_count,) + intersection_faces.shape[1:]),
            got_marks.reshape((slot_count,) + face_peaks.shape[1:]),
            wanted_ids.reshape(slot_count),
        ),
    )
    returned = lax.all_to_all(
        slot_scores.reshape(tile_count, capacity, windows, peak_count),
        "tile",
        split_axis=0,
        concat_axis=0,
        tiled=True,
    )
    fine_scores = returned.reshape(slot_count, windows, peak_count)[slot_of]
    coarse_real, coarse_imag = spectrum(coarse)
    wanted_tile = target * tile_dev + partner // per_tile
    shard_rows = lax.all_gather(coarse, "tile", axis=0, tiled=True)
    row_count = shard_rows.shape[0]
    def coarse_one(packed):
        tile_slot, wanted, mark_in = packed
        other_tile = lax.dynamic_index_in_dim(
            shard_rows, jnp.clip(wanted, 0, row_count - 1), keepdims=False
        )
        return correlate(
            (coarse_real[tile_slot], coarse_imag[tile_slot]), spectrum(other_tile), mark_in
        )

    coarse_scores = lax.map(coarse_one, (face_order // per_tile, wanted_tile, coarse_peaks))
    lower_in = from_behind(lower_faces, "sec", 1)
    section_marks = section_peaks[:, None]
    section_scores = correlate(spectrum(upper_faces), spectrum(lower_in), section_marks)
    return (fine_scores, coarse_scores, section_scores)


def np_tables(n):
    index = np.arange(n)
    angles = ((index[:, None] * index[None, :]) % n).astype(np.float32) * np.float32(TWO_PI / n)
    return np.cos(angles), np.sin(angles)


def split_tables(n, parts):
    cosine, sine = np_tables(n)
    rows = n // 2 // parts
    slots = sine[: n // 2].copy()
    slots[0] = cosine[n // 2]
    first = np.concatenate(
        [cosine[: n // 2].reshape(parts, rows, n), slots.reshape(parts, rows, n)], axis=1
    ).reshape(n, n)
    second = np.concatenate([cosine, sine], axis=1)
    marks = np.zeros((parts, 2, n, 2 * (rows + 8)), np.float32)
    for part in range(parts):
        bins = list(range(part * rows, (part + 1) * rows))
        weight = np.array([1.0 if k == 0 else 2.0 for k in bins] + [1.0 if part == 0 else 0.0] + [0.0] * 7)
        bins = bins + [n // 2] * 8
        c, s = cosine[bins].T * weight, sine[bins].T * weight
        marks[part, 0] = np.concatenate([c, -s], axis=1)
        marks[part, 1] = np.concatenate([s, c], axis=1)
    return [bf16(first), bf16(second), bf16(marks)]


def whole_tables(n):
    cosine, sine = np_tables(n)
    rows = n // 2 + 8
    first = np.concatenate([cosine[:rows], sine[:rows]], axis=0)
    weight = np.array([1.0] + [2.0] * (n // 2 - 1) + [1.0] + [0.0] * 7)
    c, s = cosine[:rows].T * weight, sine[:rows].T * weight
    marks = np.stack([np.concatenate([c, -s], axis=1), np.concatenate([s, c], axis=1)])
    return [bf16(first), bf16(marks), np.tile(weight[:, None], (1, n)).astype(np.float32)]


def bf16(table):
    return table.astype(np.float32).astype(ml_dtypes.bfloat16)


def hann(n):
    x = np.arange(n, dtype=np.float32)
    values = (0.5 - 0.5 * np.cos((x + np.float32(0.5)) * np.float32(TWO_PI / n))).astype(np.float32)
    return [values[:, None], values[None, :]]


def iota(shape, axis):
    return lax.broadcasted_iota(jnp.int32, shape, axis)


def mm(a, b):
    return jnp.dot(a, b, preferred_element_type=jnp.float32)


def pick(onehot, table):
    return lax.dot_general(
        onehot, table, (((0,), (0,)), ((), ())), preferred_element_type=jnp.float32
    )


def fold(value):
    total = value[:, :LANES]
    for start in range(LANES, value.shape[1], LANES):
        total = total + value[:, start : start + LANES]
    return total


def windowed(image, column, row):
    return (image.astype(jnp.float32) * column * row).astype(jnp.bfloat16)


def cross(ar, ai, br, bi):
    xr = ar * br + ai * bi
    xi = ai * br - ar * bi
    power = xr * xr + xi * xi
    inverse = lax.rsqrt(jnp.maximum(power, 1e-37))
    return xr, xi, inverse, power * inverse


def to_row(column, shift):
    shape = (column.shape[0], LANES)
    here = iota(shape, 1) == iota(shape, 0) + shift
    return jnp.sum(jnp.where(here, column, 0.0), axis=0, keepdims=True)


def to_grid(rows, shift, count):
    shape = (8, LANES)
    kept = jnp.where(iota(shape, 1) // count == iota(shape, 0) + shift, rows, 0.0)
    chosen = (iota((LANES, count), 0) % count == iota((LANES, count), 1)).astype(jnp.float32)
    return jnp.dot(kept, chosen, precision=lax.Precision.HIGHEST, preferred_element_type=jnp.float32)


def kernel(
    T, NS,
    ints, faces, coarse, upper, lower,
    f_col, f_row, c_col, c_row, f_first, f_second, f_marks, c_first, c_second, c_marks,
    s_first, s_marks, s_weight,
    fine_out, coarse_out, section_out,
    ints_all, ints_sm, low, f_send, f_all, c_send, c_all,
    f_sr, f_si, c_sr, c_si, f_xr, f_xi, f_in, c_xr, c_xi, c_in,
    f_a, f_cs, c_a, c_cs, f_sums, c_sums, f_msg, c_msg, f_tot, c_tot, f_it, c_it,
    f_part, c_part, out_msg, out_all,
    send_sems, recv_sems, low_sems, local_sem,
):
    me, sec = lax.axis_index("tile"), lax.axis_index("sec")
    FD, TD = faces.shape[0], coarse.shape[0]
    per_tile = FD // TD
    PK = fine_out.shape[1]
    pairs = T * FD
    barrier = pltpu.get_barrier_semaphore()
    for step in range(1, T):
        pl.semaphore_signal(barrier, inc=1, device_id={"tile": lax.rem(me + step, T)}, device_id_type=MESH)

    @pl.when(sec < NS - 1)
    def _():
        pl.semaphore_signal(barrier, inc=1, device_id={"sec": sec + 1}, device_id_type=MESH)

    @pl.when(sec > 0)
    def _():
        pl.semaphore_signal(barrier, inc=1, device_id={"sec": sec - 1}, device_id_type=MESH)

    def exchange(kind, step, source, landing):
        peer = lax.rem(me + step, T)
        return pltpu.make_async_remote_copy(
            src_ref=source(peer), dst_ref=landing.at[me], send_sem=send_sems.at[kind, step],
            recv_sem=recv_sems.at[kind, me], device_id={"tile": peer}, device_id_type=MESH,
        )

    def start(kind, source, landing):
        for step in range(1, T):
            exchange(kind, step, source, landing).start()

    def arrive(kind, source, landing):
        for step in range(1, T):
            peer = lax.rem(me + step, T)
            pltpu.make_async_remote_copy(
                src_ref=source(peer), dst_ref=landing.at[peer], send_sem=send_sems.at[kind, step],
                recv_sem=recv_sems.at[kind, peer], device_id={"tile": peer}, device_id_type=MESH,
            ).wait_recv()

    def sent(kind, source, landing):
        for step in range(1, T):
            exchange(kind, step, source, landing).wait_send()

    def lower_copy():
        return pltpu.make_async_remote_copy(
            src_ref=lower, dst_ref=low, send_sem=low_sems.at[0], recv_sem=low_sems.at[1],
            device_id={"sec": lax.rem(sec + 1, NS)}, device_id_type=MESH,
        )

    def first_step(images, col, row, table, out, count):
        n = images.shape[-1]
        for which in range(count):
            got = mm(table[...], windowed(images[which], col[...], row[...]))
            out[:, which] = got.astype(jnp.bfloat16).reshape(T, n // T, n)

    first_step(faces, f_col, f_row, f_first, f_send, FD)

    @pl.when((sec > 0) & (sec < NS - 1))
    def _():
        pl.semaphore_wait(barrier, T + 1)

    @pl.when((sec == 0) | (sec == NS - 1))
    def _():
        pl.semaphore_wait(barrier, T - 1 + (1 if NS > 1 else 0))

    sources = [lambda peer: ints, lambda peer: f_send.at[peer], lambda peer: c_send.at[peer],
               lambda peer: f_msg, lambda peer: c_msg, lambda peer: out_msg.at[peer]]
    landings = [ints_all, f_all, c_all, f_tot, c_tot, out_all]
    start(0, sources[0], landings[0])
    start(1, sources[1], landings[1])

    @pl.when(sec < NS - 1)
    def _():
        lower_copy().start()

    first_step(coarse, c_col, c_row, c_first, c_send, TD)
    start(2, sources[2], landings[2])
    ints_all[me] = ints[...]
    f_all[me] = f_send[me]
    c_all[me] = c_send[me]

    arrive(0, sources[0], landings[0])
    to_scalar = pltpu.make_async_copy(ints_all, ints_sm, local_sem)
    to_scalar.start()

    def tables_of(row, n, second, marks, a, cs, at):
        onehot = jnp.where(iota((n, LANES), 0) == row, 1.0, 0.0).astype(jnp.bfloat16)
        half = FD * PK
        width = 2 * n
        cs[pl.ds(at, FD)] = pick(onehot, second)[half:].reshape(FD, PK, width)
        for side in range(2):
            a[pl.ds(at, FD), side * PK : (side + 1) * PK, :] = pick(onehot, marks[side])[:half].reshape(FD, PK, -1)

    def peaks_from(j, _):
        rows = ints_all[j]
        tables_of(rows[0:1], f_row.shape[1], f_second[...], f_marks[me], f_a, f_cs, j * FD)
        tables_of(rows[1:2], c_row.shape[1], c_second[...], c_marks[me], c_a, c_cs, j * FD)
        return 0

    lax.fori_loop(0, T, peaks_from, 0)

    @pl.when(sec > 0)
    def _():
        lower_copy().wait_recv()

    @pl.when(sec == 0)
    def _():
        low[...] = jnp.zeros_like(low)

    n = f_row.shape[1]
    rows_s = n // 2 + 8

    def spectrum_s(image):
        got = mm(s_first[...], windowed(image, f_col[...], f_row[...])).astype(jnp.bfloat16)
        both = mm(got, f_second[...])
        p, q = both[:rows_s], both[rows_s:]
        return p[:, :n] - q[:, n:], -(p[:, n:] + q[:, :n])

    onehot = jnp.where(iota((n, LANES), 0) == ints[3:4], 1.0, 0.0).astype(jnp.bfloat16)
    cs_s = pick(onehot, f_second[...])[TD * PK : 2 * TD * PK]
    a_s = [pick(onehot, s_marks[side])[: TD * PK] for side in range(2)]
    columns = []
    for which in range(TD):
        ar, ai = spectrum_s(upper[which])
        br, bi = spectrum_s(low[which])
        xr, xi, inverse, size = cross(ar, ai, br, bi)
        total = jnp.sum(jnp.sum(size * s_weight[...], axis=0, keepdims=True), axis=1, keepdims=True)
        scale = jnp.minimum(inverse, 1.0 / (total * (0.05 / (n * n)) + 1e-6))
        unit = jnp.concatenate([xr * scale, xi * scale], axis=0).astype(jnp.bfloat16)
        at = slice(which * PK, (which + 1) * PK)
        fr = mm(a_s[0][at].astype(jnp.bfloat16), unit)
        fi = mm(a_s[1][at].astype(jnp.bfloat16), unit)
        columns.append(jnp.sum(fr * cs_s[at, :n] - fi * cs_s[at, n:], axis=1, keepdims=True))
    row = to_row(jnp.concatenate(columns, axis=0), 0)
    section_out[...] = to_grid(jnp.broadcast_to(row, (8, LANES)), 0, PK)[:TD] * (1.0 / n)

    to_scalar.wait()

    def second_step(block, n, second, sr, si, groups):
        rows = n // 2 // T
        per = T // groups
        images = block.shape[1]
        for group in range(groups):
            x = block[group * per : (group + 1) * per].reshape(per * images * 2 * rows, n)
            both = mm(x, second[...]).reshape(per * images, 2 * rows, 2 * n)
            p, q = both[:, :rows], both[:, rows:]
            special = (iota((1, rows, 1), 1) == 0) & (me == 0)
            at = slice(group * per * images, (group + 1) * per * images)
            sr[at, :rows, :] = p[:, :, :n] - jnp.where(special, 0.0, q[:, :, n:])
            si[at, :rows, :] = -(p[:, :, n:] + jnp.where(special, 0.0, q[:, :, :n]))
            sr[at, rows:, :] = q[:, :8, :n]
            si[at, rows:, :] = -q[:, :8, n:]

    def weights(rows, n):
        at = iota((rows + 8, n), 0)
        main = jnp.where((at == 0) & (me == 0), 1.0, 2.0)
        extra = jnp.where((at == rows) & (me == 0), 1.0, 0.0)
        return jnp.where(at < rows, main, extra)

    def cross_all(n, sr, si, xr, xi, inv, sums, own_of, other_of, msg):
        w = weights(n // 2 // T, n)

        def one(p, _):
            own, other = own_of(p), other_of(p)
            vr, vi, inverse, size = cross(sr[own], si[own], sr[other], si[other])
            xr[p], xi[p], inv[p] = vr, vi, inverse
            sums[pl.ds(p, 1), :] = fold(jnp.sum(size * w, axis=0, keepdims=True))
            return 0

        lax.fori_loop(0, pairs, one, 0, unroll=4)
        total = jnp.sum(sums[...], axis=1, keepdims=True)
        msg[...] = jnp.broadcast_to(to_row(total, 0), msg.shape)

    def score_all(n, tot, it, xr, xi, inv, a, cs, part):
        row = jnp.sum(tot[...], axis=0)[0:1]
        limit = 1.0 / (row * (0.05 / (n * n)) + 1e-6)
        shape = (pairs, LANES)
        column = jnp.sum(jnp.where(iota(shape, 1) == iota(shape, 0), limit, 0.0), axis=1, keepdims=True)
        it[...] = jnp.broadcast_to(column, it.shape)

        def one(p, _):
            scale = jnp.minimum(inv[p], it[pl.ds(p, 1), :])
            unit = jnp.concatenate([xr[p] * scale, xi[p] * scale], axis=0).astype(jnp.bfloat16)
            got = mm(a[p].astype(jnp.bfloat16), unit)
            table = cs[p]
            part[p] = fold(got[:PK] * table[:, :n] - got[PK:] * table[:, n:])
            return 0

        lax.fori_loop(0, pairs, one, 0, unroll=4)

    NF, NC = f_row.shape[1], c_row.shape[1]
    arrive(1, sources[1], landings[1])
    second_step(f_all, NF, f_second, f_sr, f_si, 2)
    cross_all(
        NF, f_sr, f_si, f_xr, f_xi, f_in, f_sums, lambda p: p,
        lambda p: ints_sm[p // FD, 2, p % FD] * FD + ints_sm[p // FD, 2, FD + p % FD], f_msg,
    )
    start(3, sources[3], landings[3])
    f_tot[me] = f_msg[...]
    arrive(2, sources[2], landings[2])
    second_step(c_all, NC, c_second, c_sr, c_si, 2)
    cross_all(
        NC, c_sr, c_si, c_xr, c_xi, c_in, c_sums, lambda p: p // per_tile,
        lambda p: ints_sm[p // FD, 2, p % FD] * TD + ints_sm[p // FD, 2, FD + p % FD] // per_tile, c_msg,
    )
    start(4, sources[4], landings[4])
    c_tot[me] = c_msg[...]
    arrive(3, sources[3], landings[3])
    score_all(NF, f_tot, f_it, f_xr, f_xi, f_in, f_a, f_cs, f_part)
    arrive(4, sources[4], landings[4])
    score_all(NC, c_tot, c_it, c_xr, c_xi, c_in, c_a, c_cs, c_part)

    def gather(j, _):
        def column(part):
            block = part[pl.ds(j * FD, FD)].reshape(FD * PK, LANES)
            return jnp.sum(block, axis=1, keepdims=True)

        row = to_row(column(c_part), 0) + to_row(column(f_part), FD * PK)
        out_msg[j] = jnp.broadcast_to(row, (8, LANES))
        return 0

    lax.fori_loop(0, T, gather, 0)
    start(5, sources[5], landings[5])
    out_all[me] = out_msg[me]
    for kind in range(5):
        sent(kind, sources[kind], landings[kind])

    @pl.when(sec < NS - 1)
    def _():
        lower_copy().wait_send()

    arrive(5, sources[5], landings[5])
    total = jnp.sum(out_all[...], axis=0)
    coarse_out[...] = to_grid(total, 0, PK) * (1.0 / NC)
    fine_out[...] = to_grid(total, FD, PK) * (1.0 / NF)
    sent(5, sources[5], landings[5])


def split_body(
    T, NS, intersection_faces, destination, partner, face_peaks, coarse, coarse_peaks,
    upper_faces, lower_faces, section_peaks,
):
    FD, TD, PK = intersection_faces.shape[0], coarse.shape[0], face_peaks.shape[2]
    NF, NC = intersection_faces.shape[-1], coarse.shape[-1]
    pairs = T * FD

    def line(*parts):
        flat = jnp.concatenate([part.reshape(-1) for part in parts])
        return jnp.pad(flat, (0, LANES - flat.shape[0]))

    ints = jnp.stack([
        line(face_peaks[:, 0], face_peaks[:, 1]),
        line(coarse_peaks[:, 0], coarse_peaks[:, 1]),
        line(destination, partner),
        line(section_peaks[:, 0], section_peaks[:, 1]),
    ] + [jnp.zeros((LANES,), jnp.int32)] * 4)
    operands = [
        ints, intersection_faces.reshape(FD, NF, NF), coarse,
        upper_faces.reshape(TD, NF, NF), lower_faces.reshape(TD, NF, NF),
    ] + [jnp.asarray(t) for t in (
        hann(NF) + hann(NC) + split_tables(NF, T) + split_tables(NC, T) + whole_tables(NF)
    )]
    fr, cr = NF // 2 // T + 8, NC // 2 // T + 8
    f32 = jnp.float32
    V = pltpu.VMEM
    scratch = [
        V((T, 8, LANES), jnp.int32), pltpu.SMEM((T, 8, LANES), jnp.int32),
        V((TD, NF, NF), jnp.bfloat16),
        V((T, FD, NF // T, NF), jnp.bfloat16), V((T, FD, NF // T, NF), jnp.bfloat16),
        V((T, TD, NC // T, NC), jnp.bfloat16), V((T, TD, NC // T, NC), jnp.bfloat16),
        V((pairs, fr, NF), f32), V((pairs, fr, NF), f32),
        V((T * TD, cr, NC), f32), V((T * TD, cr, NC), f32),
    ] + [V((pairs, fr, NF), f32)] * 3 + [V((pairs, cr, NC), f32)] * 3 + [
        V((pairs, 2 * PK, 2 * fr), f32), V((pairs, PK, 2 * NF), f32),
        V((pairs, 2 * PK, 2 * cr), f32), V((pairs, PK, 2 * NC), f32),
        V((pairs, LANES), f32), V((pairs, LANES), f32),
        V((8, LANES), f32), V((8, LANES), f32),
        V((T, 8, LANES), f32), V((T, 8, LANES), f32),
        V((pairs, NF), f32), V((pairs, NC), f32),
        V((pairs, PK, LANES), f32), V((pairs, PK, LANES), f32),
        V((T, 8, LANES), f32), V((T, 8, LANES), f32),
        pltpu.SemaphoreType.DMA((6, T)), pltpu.SemaphoreType.DMA((6, T)),
        pltpu.SemaphoreType.DMA((2,)), pltpu.SemaphoreType.DMA,
    ]
    fine, coarse_scores, section = pl.pallas_call(
        functools.partial(kernel, T, NS),
        out_shape=(
            jax.ShapeDtypeStruct((FD, PK), f32), jax.ShapeDtypeStruct((FD, PK), f32),
            jax.ShapeDtypeStruct((TD, PK), f32),
        ),
        in_specs=[pl.BlockSpec(memory_space=pltpu.VMEM)] * len(operands),
        out_specs=(pl.BlockSpec(memory_space=pltpu.VMEM),) * 3,
        scratch_shapes=scratch,
        compiler_params=pltpu.CompilerParams(
            collective_id=0, has_side_effects=True, vmem_limit_bytes=44 * 1024 * 1024
        ),
    )(*operands)
    return fine.reshape(FD, 1, PK), coarse_scores, section.reshape(TD, 1, PK)


def choose(T, NS, *args):
    faces, coarse, peaks = args[0], args[4], args[3]
    fits = (
        faces.shape[1] == 1
        and peaks.shape[2] == 8
        and faces.shape[0] == 8
        and faces.shape[-1] // 2 % (8 * T) == 0
        and coarse.shape[-1] // 2 % (8 * T) == 0
        and T * faces.shape[0] <= LANES
    )
    return split_body(T, NS, *args) if fits else body(*args)


def solution(mesh):
    return jax.shard_map(
        functools.partial(choose, mesh.shape["tile"], mesh.shape["sec"]),
        mesh=mesh,
        in_specs=(
            P(("sec", "tile"), None, None, None),
            P(("sec", "tile"), None),
            P(("sec", "tile")),
            P(("sec", "tile"), None, None),
            P(("sec", "tile"), None, None),
            P(("sec", "tile"), None, None),
            P(("sec", "tile"), None, None, None),
            P(("sec", "tile"), None, None, None),
            P(("sec", "tile"), None, None),
        ),
        out_specs=(
            P(("sec", "tile"), None, None),
            P(("sec", "tile"), None),
            P(("sec", "tile"), None, None),
        ),
        check_vma=False,
    )
```

```python
import functools

import jax
import jax.numpy as jnp
import ml_dtypes
import numpy as np
from jax import lax
from jax.experimental import pallas as pl
from jax.experimental.pallas import tpu as pltpu
from jax.sharding import PartitionSpec as P

TWO_PI = 6.283185307179586
LANES = 128
MESH = pl.DeviceIdType.MESH


def from_behind(value, axis, steps):
    count = lax.axis_size(axis)
    first, last = (max(0, -steps), min(count, count - steps))
    return lax.ppermute(value, axis, [(source, source + steps) for source in range(first, last)])


def window_weights(extent):
    positions = jnp.arange(extent, dtype=jnp.float32)
    return 0.5 - 0.5 * jnp.cos((positions + 0.5) * (TWO_PI / extent))


def dft_tables(extent):
    indices = jnp.arange(extent, dtype=jnp.int32)
    angles = (indices[:, None] * indices[None, :] % extent).astype(jnp.float32) * (TWO_PI / extent)
    return (jnp.cos(angles).astype(jnp.bfloat16), jnp.sin(angles).astype(jnp.bfloat16))


def spectrum(images):
    extent = images.shape[-1]
    weights = window_weights(extent)
    shaped = (images.astype(jnp.float32) * weights[:, None] * weights[None, :]).astype(jnp.bfloat16)
    cosine, sine_table = dft_tables(extent)
    segment_tables = jnp.stack([cosine, sine_table])
    segment_one = jnp.einsum(
        "jkx,...xy->...jky", segment_tables, shaped, preferred_element_type=jnp.float32
    ).astype(jnp.bfloat16)
    second_tables = jnp.stack(
        [
            jnp.concatenate([cosine, sine_table], axis=1),
            jnp.concatenate([-sine_table, cosine], axis=1),
        ]
    )
    segment_two = jnp.einsum(
        "...jky,jyl->...kl", segment_one, second_tables, preferred_element_type=jnp.float32
    )
    return (segment_two[..., :extent], -segment_two[..., extent:])


def correlate(own_spec, other_spec, peak_marks):
    own_real, own_imag = own_spec
    other_real, other_imag = other_spec
    cross_real = own_real * other_real + own_imag * other_imag
    cross_imag = own_imag * other_real - own_real * other_imag
    magnitude = jnp.sqrt(cross_real * cross_real + cross_imag * cross_imag)
    floor_value = 0.05 * jnp.mean(magnitude, axis=(-2, -1), keepdims=True) + 1e-06
    divisor = jnp.maximum(magnitude, floor_value)
    unit_real = cross_real / divisor
    unit_imag = cross_imag / divisor
    extent = own_real.shape[-1]
    indices = jnp.arange(extent, dtype=jnp.int32)
    row_angles = (peak_marks[..., 0, :, None] * indices % extent).astype(jnp.float32) * (
        TWO_PI / extent
    )
    col_angles = (peak_marks[..., 1, :, None] * indices % extent).astype(jnp.float32) * (
        TWO_PI / extent
    )
    row_cos = jnp.cos(row_angles)
    row_sin = jnp.sin(row_angles)
    high = lax.Precision.HIGHEST
    first_real = jnp.einsum("...pk,...kl->...pl", row_cos, unit_real, precision=high) - jnp.einsum(
        "...pk,...kl->...pl", row_sin, unit_imag, precision=high
    )
    first_imag = jnp.einsum("...pk,...kl->...pl", row_cos, unit_imag, precision=high) + jnp.einsum(
        "...pk,...kl->...pl", row_sin, unit_real, precision=high
    )
    return (
        jnp.sum(first_real * jnp.cos(col_angles) - first_imag * jnp.sin(col_angles), axis=-1)
        / extent
    )


def body(
    intersection_faces,
    destination,
    partner,
    face_peaks,
    coarse,
    coarse_peaks,
    upper_faces,
    lower_faces,
    section_peaks,
):
    face_dev = intersection_faces.shape[0]
    tile_dev = coarse.shape[0]
    per_tile = face_dev // tile_dev
    windows = intersection_faces.shape[1]
    peak_count = face_peaks.shape[2]
    tile_count = lax.axis_size("tile")
    capacity = max(2, (face_dev + tile_count - 1) // tile_count)
    slot_count = tile_count * capacity
    target = destination[:, 0]
    face_order = jnp.arange(face_dev, dtype=jnp.int32)
    earlier = (target[None, :] == target[:, None]) & (face_order[None, :] < face_order[:, None])
    position = jnp.sum(earlier.astype(jnp.int32), axis=1)
    slot_of = target * capacity + position
    slot_match = slot_of[None, :] == jnp.arange(slot_count, dtype=jnp.int32)[:, None]
    filled = jnp.any(slot_match, axis=1)
    source = jnp.sum(jnp.where(slot_match, face_order[None, :], 0), axis=1)
    requests = jnp.where(filled, partner[source] + 1, 0).reshape(tile_count, capacity)
    own_real, own_imag = spectrum(intersection_faces)
    parcel = jnp.einsum(
        "sf,fwxy->swxy", slot_match.astype(jnp.bfloat16), intersection_faces,
        preferred_element_type=jnp.float32,
    ).astype(jnp.bfloat16)
    parcel = parcel.reshape((tile_count, capacity) + intersection_faces.shape[1:])
    peak_marks = jnp.sum(
        jnp.where(slot_match[:, :, None, None], face_peaks[None], 0), axis=1
    ).reshape((tile_count, capacity) + face_peaks.shape[1:])
    got_faces, got_marks, wanted_ids = (
        lax.all_to_all(parcel, "tile", split_axis=0, concat_axis=0, tiled=True),
        lax.all_to_all(peak_marks, "tile", split_axis=0, concat_axis=0, tiled=True),
        lax.all_to_all(requests, "tile", split_axis=0, concat_axis=0, tiled=True),
    )

    def one_slot(packed):
        face_in, mark_in, wanted = packed
        chosen_slot = jnp.maximum(wanted - 1, 0)
        own_part = (own_real[chosen_slot], own_imag[chosen_slot])
        marks_all = mark_in[None]
        scores = correlate(spectrum(face_in), own_part, marks_all)
        return jnp.where(wanted > 0, scores, jnp.zeros_like(scores))

    slot_scores = lax.map(
        one_slot,
        (
            got_faces.reshape((slot_count,) + intersection_faces.shape[1:]),
            got_marks.reshape((slot_count,) + face_peaks.shape[1:]),
            wanted_ids.reshape(slot_count),
        ),
    )
    returned = lax.all_to_all(
        slot_scores.reshape(tile_count, capacity, windows, peak_count),
        "tile",
        split_axis=0,
        concat_axis=0,
        tiled=True,
    )
    fine_scores = returned.reshape(slot_count, windows, peak_count)[slot_of]
    coarse_real, coarse_imag = spectrum(coarse)
    wanted_tile = target * tile_dev + partner // per_tile
    shard_rows = lax.all_gather(coarse, "tile", axis=0, tiled=True)
    row_count = shard_rows.shape[0]
    def coarse_one(packed):
        tile_slot, wanted, mark_in = packed
        other_tile = lax.dynamic_index_in_dim(
            shard_rows, jnp.clip(wanted, 0, row_count - 1), keepdims=False
        )
        return correlate(
            (coarse_real[tile_slot], coarse_imag[tile_slot]), spectrum(other_tile), mark_in
        )

    coarse_scores = lax.map(coarse_one, (face_order // per_tile, wanted_tile, coarse_peaks))
    lower_in = from_behind(lower_faces, "sec", 1)
    section_marks = section_peaks[:, None]
    section_scores = correlate(spectrum(upper_faces), spectrum(lower_in), section_marks)
    return (fine_scores, coarse_scores, section_scores)


def np_tables(n):
    index = np.arange(n)
    angles = ((index[:, None] * index[None, :]) % n).astype(np.float32) * np.float32(TWO_PI / n)
    return np.cos(angles), np.sin(angles)


def split_tables(n, parts):
    cosine, sine = np_tables(n)
    rows = n // 2 // parts
    slots = sine[: n // 2].copy()
    slots[0] = cosine[n // 2]
    first = np.concatenate(
        [cosine[: n // 2].reshape(parts, rows, n), slots.reshape(parts, rows, n)], axis=1
    ).reshape(n, n)
    second = np.concatenate([cosine, sine], axis=1)
    marks = np.zeros((parts, 2, n, 2 * (rows + 8)), np.float32)
    for part in range(parts):
        bins = list(range(part * rows, (part + 1) * rows))
        weight = np.array([1.0 if k == 0 else 2.0 for k in bins] + [1.0 if part == 0 else 0.0] + [0.0] * 7)
        bins = bins + [n // 2] * 8
        c, s = cosine[bins].T * weight, sine[bins].T * weight
        marks[part, 0] = np.concatenate([c, -s], axis=1)
        marks[part, 1] = np.concatenate([s, c], axis=1)
    return [bf16(first), bf16(second), bf16(marks)]


def whole_tables(n):
    cosine, sine = np_tables(n)
    rows = n // 2 + 8
    first = np.concatenate([cosine[:rows], sine[:rows]], axis=0)
    weight = np.array([1.0] + [2.0] * (n // 2 - 1) + [1.0] + [0.0] * 7)
    c, s = cosine[:rows].T * weight, sine[:rows].T * weight
    marks = np.stack([np.concatenate([c, -s], axis=1), np.concatenate([s, c], axis=1)])
    return [bf16(first), bf16(marks), np.tile(weight[:, None], (1, n)).astype(np.float32)]


def bf16(table):
    return table.astype(np.float32).astype(ml_dtypes.bfloat16)


def hann(n):
    x = np.arange(n, dtype=np.float32)
    values = (0.5 - 0.5 * np.cos((x + np.float32(0.5)) * np.float32(TWO_PI / n))).astype(np.float32)
    return [values[:, None], values[None, :]]


def iota(shape, axis):
    return lax.broadcasted_iota(jnp.int32, shape, axis)


def mm(a, b):
    return jnp.dot(a, b, preferred_element_type=jnp.float32)


def pick(onehot, table):
    return lax.dot_general(
        onehot, table, (((0,), (0,)), ((), ())), preferred_element_type=jnp.float32
    )


def fold(value):
    total = value[:, :LANES]
    for start in range(LANES, value.shape[1], LANES):
        total = total + value[:, start : start + LANES]
    return total


def windowed(image, column, row):
    return (image.astype(jnp.float32) * column * row).astype(jnp.bfloat16)


def cross(ar, ai, br, bi):
    xr = ar * br + ai * bi
    xi = ai * br - ar * bi
    power = xr * xr + xi * xi
    inverse = lax.rsqrt(jnp.maximum(power, 1e-37))
    return xr, xi, inverse, power * inverse


def to_row(column, shift):
    shape = (column.shape[0], LANES)
    here = iota(shape, 1) == iota(shape, 0) + shift
    return jnp.sum(jnp.where(here, column, 0.0), axis=0, keepdims=True)


def to_grid(rows, shift, count):
    shape = (8, LANES)
    kept = jnp.where(iota(shape, 1) // count == iota(shape, 0) + shift, rows, 0.0)
    chosen = (iota((LANES, count), 0) % count == iota((LANES, count), 1)).astype(jnp.float32)
    return jnp.dot(kept, chosen, precision=lax.Precision.HIGHEST, preferred_element_type=jnp.float32)


def kernel(
    T, NS, h_dest, h_part, h_fp, h_cp, h_sp, h_faces, h_coarse, h_upper, lower,
    h_f_col, h_f_row, h_c_col, h_c_row, h_f_first, h_f_second, h_f_marks,
    h_c_first, h_c_second, h_c_marks, h_s_first, h_s_marks, h_s_weight,
    fine_out, coarse_out, section_out,
    dest, part, fp, cp, sp, faces, coarse, upper, f_col, f_row, c_col, c_row,
    f_first, f_second, f_marks, c_first, c_second, c_marks, s_first, s_marks, s_weight,
    load_sems, ints, ints_all, ints_sm, low, f_send, f_all, c_send, c_all,
    f_sr, f_si, c_sr, c_si, f_xr, f_xi, f_in, c_xr, c_xi, c_in,
    f_a, f_cs, c_a, c_cs, f_sums, c_sums, f_msg, c_msg, f_tot, c_tot, f_it, c_it,
    f_part, c_part, out_msg, out_all,
    send_sems, recv_sems, low_sems, local_sem,
):
    me, sec = lax.axis_index("tile"), lax.axis_index("sec")
    loads = [
        pltpu.make_async_copy(source, target, load_sems.at[index])
        for index, (source, target) in enumerate([
            (h_f_col, f_col), (h_f_row, f_row), (h_f_first, f_first), (h_faces, faces),
            (h_dest, dest), (h_part, part), (h_fp, fp), (h_cp, cp), (h_sp, sp),
            (h_c_col, c_col), (h_c_row, c_row), (h_c_first, c_first), (h_coarse, coarse),
            (h_f_second, f_second), (h_f_marks.at[me], f_marks),
            (h_c_second, c_second), (h_c_marks.at[me], c_marks),
            (h_upper, upper), (h_s_first, s_first), (h_s_marks, s_marks), (h_s_weight, s_weight),
        ])
    ]
    for load in loads:
        load.start()

    def loaded(low_at, high_at):
        for load in loads[low_at:high_at]:
            load.wait()

    FD, TD = faces.shape[0], coarse.shape[0]
    per_tile = FD // TD
    PK = fine_out.shape[1]
    pairs = T * FD
    barrier = pltpu.get_barrier_semaphore()
    for step in range(1, T):
        pl.semaphore_signal(barrier, inc=1, device_id={"tile": lax.rem(me + step, T)}, device_id_type=MESH)

    @pl.when(sec < NS - 1)
    def _():
        pl.semaphore_signal(barrier, inc=1, device_id={"sec": sec + 1}, device_id_type=MESH)

    @pl.when(sec > 0)
    def _():
        pl.semaphore_signal(barrier, inc=1, device_id={"sec": sec - 1}, device_id_type=MESH)

    def exchange(kind, step, source, landing):
        peer = lax.rem(me + step, T)
        return pltpu.make_async_remote_copy(
            src_ref=source(peer), dst_ref=landing.at[me], send_sem=send_sems.at[kind, step],
            recv_sem=recv_sems.at[kind, me], device_id={"tile": peer}, device_id_type=MESH,
        )

    def start(kind, source, landing):
        for step in range(1, T):
            exchange(kind, step, source, landing).start()

    def arrive(kind, source, landing):
        for step in range(1, T):
            peer = lax.rem(me + step, T)
            pltpu.make_async_remote_copy(
                src_ref=source(peer), dst_ref=landing.at[peer], send_sem=send_sems.at[kind, step],
                recv_sem=recv_sems.at[kind, peer], device_id={"tile": peer}, device_id_type=MESH,
            ).wait_recv()

    def sent(kind, source, landing):
        for step in range(1, T):
            exchange(kind, step, source, landing).wait_send()

    def lower_copy():
        return pltpu.make_async_remote_copy(
            src_ref=lower, dst_ref=low, send_sem=low_sems.at[0], recv_sem=low_sems.at[1],
            device_id={"sec": lax.rem(sec + 1, NS)}, device_id_type=MESH,
        )

    def first_step(images, col, row, table, out, count):
        n = images.shape[-1]
        for which in range(count):
            got = mm(table[...], windowed(images[which], col[...], row[...]))
            out[:, which] = got.astype(jnp.bfloat16).reshape(T, n // T, n)

    def lanes_of(grid, shift):
        count, width = grid.shape
        chosen = iota((width, LANES), 1) % width == iota((width, LANES), 0)
        spread = mm(grid.astype(jnp.float32).astype(jnp.bfloat16), chosen.astype(jnp.float32).astype(jnp.bfloat16))
        shape = (count, LANES)
        kept = iota(shape, 1) // width == iota(shape, 0) + shift
        return jnp.sum(jnp.where(kept, spread, 0.0), axis=0, keepdims=True)

    loaded(4, 9)
    lines = [
        lanes_of(fp[:, 0, :], 0) + lanes_of(fp[:, 1, :], FD),
        lanes_of(cp[:, 0, :], 0) + lanes_of(cp[:, 1, :], FD),
        lanes_of(sp[:, 0, :], 0) + lanes_of(sp[:, 1, :], TD),
    ]
    lines = jnp.concatenate(lines + [jnp.zeros((5, LANES), jnp.float32)], axis=0)
    ints[...] = (lines + 0.5).astype(jnp.int32)
    ints[3:4, :FD] = dest[...]
    ints[4:5, :FD] = part[...]
    loaded(0, 4)
    first_step(faces, f_col, f_row, f_first, f_send, FD)

    @pl.when((sec > 0) & (sec < NS - 1))
    def _():
        pl.semaphore_wait(barrier, T + 1)

    @pl.when((sec == 0) | (sec == NS - 1))
    def _():
        pl.semaphore_wait(barrier, T - 1 + (1 if NS > 1 else 0))

    sources = [lambda peer: ints, lambda peer: f_send.at[peer], lambda peer: c_send.at[peer],
               lambda peer: f_msg, lambda peer: c_msg, lambda peer: out_msg.at[peer]]
    landings = [ints_all, f_all, c_all, f_tot, c_tot, out_all]
    start(0, sources[0], landings[0])
    start(1, sources[1], landings[1])

    @pl.when(sec < NS - 1)
    def _():
        lower_copy().start()

    loaded(9, 13)
    first_step(coarse, c_col, c_row, c_first, c_send, TD)
    start(2, sources[2], landings[2])
    ints_all[me] = ints[...]
    f_all[me] = f_send[me]
    c_all[me] = c_send[me]

    loaded(13, len(loads))
    arrive(0, sources[0], landings[0])
    to_scalar = pltpu.make_async_copy(ints_all, ints_sm, local_sem)
    to_scalar.start()

    def tables_of(row, n, second, marks, a, cs, at):
        onehot = jnp.where(iota((n, LANES), 0) == row, 1.0, 0.0).astype(jnp.bfloat16)
        half = FD * PK
        width = 2 * n
        cs[pl.ds(at, FD)] = pick(onehot, second)[half:].reshape(FD, PK, width)
        for side in range(2):
            a[pl.ds(at, FD), side * PK : (side + 1) * PK, :] = pick(onehot, marks[side])[:half].reshape(FD, PK, -1)

    def peaks_from(j, _):
        rows = ints_all[j]
        tables_of(rows[0:1], f_row.shape[1], f_second[...], f_marks, f_a, f_cs, j * FD)
        tables_of(rows[1:2], c_row.shape[1], c_second[...], c_marks, c_a, c_cs, j * FD)
        return 0

    lax.fori_loop(0, T, peaks_from, 0)

    @pl.when(sec > 0)
    def _():
        lower_copy().wait_recv()

    @pl.when(sec == 0)
    def _():
        low[...] = jnp.zeros_like(low)

    n = f_row.shape[1]
    rows_s = n // 2 + 8

    def spectrum_s(image):
        got = mm(s_first[...], windowed(image, f_col[...], f_row[...])).astype(jnp.bfloat16)
        both = mm(got, f_second[...])
        p, q = both[:rows_s], both[rows_s:]
        return p[:, :n] - q[:, n:], -(p[:, n:] + q[:, :n])

    onehot = jnp.where(iota((n, LANES), 0) == ints[2:3], 1.0, 0.0).astype(jnp.bfloat16)
    cs_s = pick(onehot, f_second[...])[TD * PK : 2 * TD * PK]
    a_s = [pick(onehot, s_marks[side])[: TD * PK] for side in range(2)]
    columns = []
    for which in range(TD):
        ar, ai = spectrum_s(upper[which])
        br, bi = spectrum_s(low[which])
        xr, xi, inverse, size = cross(ar, ai, br, bi)
        total = jnp.sum(jnp.sum(size * s_weight[...], axis=0, keepdims=True), axis=1, keepdims=True)
        scale = jnp.minimum(inverse, 1.0 / (total * (0.05 / (n * n)) + 1e-6))
        unit = jnp.concatenate([xr * scale, xi * scale], axis=0).astype(jnp.bfloat16)
        at = slice(which * PK, (which + 1) * PK)
        fr = mm(a_s[0][at].astype(jnp.bfloat16), unit)
        fi = mm(a_s[1][at].astype(jnp.bfloat16), unit)
        columns.append(jnp.sum(fr * cs_s[at, :n] - fi * cs_s[at, n:], axis=1, keepdims=True))
    row = to_row(jnp.concatenate(columns, axis=0), 0)
    section_out[...] = to_grid(jnp.broadcast_to(row, (8, LANES)), 0, PK)[:TD] * (1.0 / n)

    to_scalar.wait()

    def second_step(block, n, second, sr, si, groups):
        rows = n // 2 // T
        per = T // groups
        images = block.shape[1]
        for group in range(groups):
            x = block[group * per : (group + 1) * per].reshape(per * images * 2 * rows, n)
            both = mm(x, second[...]).reshape(per * images, 2 * rows, 2 * n)
            p, q = both[:, :rows], both[:, rows:]
            special = (iota((1, rows, 1), 1) == 0) & (me == 0)
            at = slice(group * per * images, (group + 1) * per * images)
            sr[at, :rows, :] = p[:, :, :n] - jnp.where(special, 0.0, q[:, :, n:])
            si[at, :rows, :] = -(p[:, :, n:] + jnp.where(special, 0.0, q[:, :, :n]))
            sr[at, rows:, :] = q[:, :8, :n]
            si[at, rows:, :] = -q[:, :8, n:]

    def weights(rows, n):
        at = iota((rows + 8, n), 0)
        main = jnp.where((at == 0) & (me == 0), 1.0, 2.0)
        extra = jnp.where((at == rows) & (me == 0), 1.0, 0.0)
        return jnp.where(at < rows, main, extra)

    def cross_all(n, sr, si, xr, xi, inv, sums, own_of, other_of, msg):
        w = weights(n // 2 // T, n)

        def one(p, _):
            own, other = own_of(p), other_of(p)
            vr, vi, inverse, size = cross(sr[own], si[own], sr[other], si[other])
            xr[p], xi[p], inv[p] = vr, vi, inverse
            sums[pl.ds(p, 1), :] = fold(jnp.sum(size * w, axis=0, keepdims=True))
            return 0

        lax.fori_loop(0, pairs, one, 0, unroll=4)
        total = jnp.sum(sums[...], axis=1, keepdims=True)
        msg[...] = jnp.broadcast_to(to_row(total, 0), msg.shape)

    def score_all(n, tot, it, xr, xi, inv, a, cs, part):
        row = jnp.sum(tot[...], axis=0)[0:1]
        limit = 1.0 / (row * (0.05 / (n * n)) + 1e-6)
        shape = (pairs, LANES)
        column = jnp.sum(jnp.where(iota(shape, 1) == iota(shape, 0), limit, 0.0), axis=1, keepdims=True)
        it[...] = jnp.broadcast_to(column, it.shape)

        def one(p, _):
            scale = jnp.minimum(inv[p], it[pl.ds(p, 1), :])
            unit = jnp.concatenate([xr[p] * scale, xi[p] * scale], axis=0).astype(jnp.bfloat16)
            got = mm(a[p].astype(jnp.bfloat16), unit)
            table = cs[p]
            part[p] = fold(got[:PK] * table[:, :n] - got[PK:] * table[:, n:])
            return 0

        lax.fori_loop(0, pairs, one, 0, unroll=4)

    NF, NC = f_row.shape[1], c_row.shape[1]
    arrive(1, sources[1], landings[1])
    second_step(f_all, NF, f_second, f_sr, f_si, 2)
    cross_all(
        NF, f_sr, f_si, f_xr, f_xi, f_in, f_sums, lambda p: p,
        lambda p: jnp.clip(ints_sm[p // FD, 3, p % FD] * FD + ints_sm[p // FD, 4, p % FD], 0, pairs - 1), f_msg,
    )
    start(3, sources[3], landings[3])
    f_tot[me] = f_msg[...]
    arrive(2, sources[2], landings[2])
    second_step(c_all, NC, c_second, c_sr, c_si, 2)
    cross_all(
        NC, c_sr, c_si, c_xr, c_xi, c_in, c_sums, lambda p: p // per_tile,
        lambda p: jnp.clip(ints_sm[p // FD, 3, p % FD] * TD + ints_sm[p // FD, 4, p % FD] // per_tile, 0, T * TD - 1), c_msg,
    )
    start(4, sources[4], landings[4])
    c_tot[me] = c_msg[...]
    arrive(3, sources[3], landings[3])
    score_all(NF, f_tot, f_it, f_xr, f_xi, f_in, f_a, f_cs, f_part)
    arrive(4, sources[4], landings[4])
    score_all(NC, c_tot, c_it, c_xr, c_xi, c_in, c_a, c_cs, c_part)

    def gather(j, _):
        def column(part):
            block = part[pl.ds(j * FD, FD)].reshape(FD * PK, LANES)
            return jnp.sum(block, axis=1, keepdims=True)

        row = to_row(column(c_part), 0) + to_row(column(f_part), FD * PK)
        out_msg[j] = jnp.broadcast_to(row, (8, LANES))
        return 0

    lax.fori_loop(0, T, gather, 0)
    start(5, sources[5], landings[5])
    out_all[me] = out_msg[me]
    for kind in range(5):
        sent(kind, sources[kind], landings[kind])

    @pl.when(sec < NS - 1)
    def _():
        lower_copy().wait_send()

    arrive(5, sources[5], landings[5])
    total = jnp.sum(out_all[...], axis=0)
    coarse_out[...] = to_grid(total, 0, PK) * (1.0 / NC)
    fine_out[...] = to_grid(total, FD, PK) * (1.0 / NF)
    sent(5, sources[5], landings[5])


def split_body(
    T, NS, intersection_faces, destination, partner, face_peaks, coarse, coarse_peaks,
    upper_faces, lower_faces, section_peaks,
):
    FD, TD, PK = intersection_faces.shape[0], coarse.shape[0], face_peaks.shape[2]
    NF, NC = intersection_faces.shape[-1], coarse.shape[-1]
    pairs = T * FD

    operands = [
        destination.reshape(1, FD), partner.reshape(1, FD), face_peaks, coarse_peaks, section_peaks,
        intersection_faces.reshape(FD, NF, NF), coarse,
        upper_faces.reshape(TD, NF, NF), lower_faces.reshape(TD, NF, NF),
    ] + [jnp.asarray(t) for t in (
        hann(NF) + hann(NC) + split_tables(NF, T) + split_tables(NC, T) + whole_tables(NF)
    )]
    fr, cr = NF // 2 // T + 8, NC // 2 // T + 8
    f32 = jnp.float32
    V = pltpu.VMEM
    kept = [(x.shape[1:] if x.ndim == 4 else x.shape, x.dtype) for x in operands]
    scratch = [V(*one) for index, one in enumerate(kept) if index != 8] + [
        pltpu.SemaphoreType.DMA((len(operands) - 1,)), V((8, LANES), jnp.int32),
        V((T, 8, LANES), jnp.int32), pltpu.SMEM((T, 8, LANES), jnp.int32),
        V((TD, NF, NF), jnp.bfloat16),
        V((T, FD, NF // T, NF), jnp.bfloat16), V((T, FD, NF // T, NF), jnp.bfloat16),
        V((T, TD, NC // T, NC), jnp.bfloat16), V((T, TD, NC // T, NC), jnp.bfloat16),
        V((pairs, fr, NF), f32), V((pairs, fr, NF), f32),
        V((T * TD, cr, NC), f32), V((T * TD, cr, NC), f32),
    ] + [V((pairs, fr, NF), f32)] * 3 + [V((pairs, cr, NC), f32)] * 3 + [
        V((pairs, 2 * PK, 2 * fr), f32), V((pairs, PK, 2 * NF), f32),
        V((pairs, 2 * PK, 2 * cr), f32), V((pairs, PK, 2 * NC), f32),
        V((pairs, LANES), f32), V((pairs, LANES), f32),
        V((8, LANES), f32), V((8, LANES), f32),
        V((T, 8, LANES), f32), V((T, 8, LANES), f32),
        V((pairs, NF), f32), V((pairs, NC), f32),
        V((pairs, PK, LANES), f32), V((pairs, PK, LANES), f32),
        V((T, 8, LANES), f32), V((T, 8, LANES), f32),
        pltpu.SemaphoreType.DMA((6, T)), pltpu.SemaphoreType.DMA((6, T)),
        pltpu.SemaphoreType.DMA((2,)), pltpu.SemaphoreType.DMA,
    ]
    fine, coarse_scores, section = pl.pallas_call(
        functools.partial(kernel, T, NS),
        out_shape=(
            jax.ShapeDtypeStruct((FD, PK), f32), jax.ShapeDtypeStruct((FD, PK), f32),
            jax.ShapeDtypeStruct((TD, PK), f32),
        ),
        in_specs=[pl.BlockSpec(memory_space=pltpu.HBM)] * len(operands),
        out_specs=(pl.BlockSpec(memory_space=pltpu.VMEM),) * 3,
        scratch_shapes=scratch,
        compiler_params=pltpu.CompilerParams(
            collective_id=0, has_side_effects=True, vmem_limit_bytes=60 * 1024 * 1024
        ),
    )(*operands)
    return fine.reshape(FD, 1, PK), coarse_scores, section.reshape(TD, 1, PK)


def choose(T, NS, *args):
    faces, coarse, peaks = args[0], args[4], args[3]
    fits = (
        faces.shape[1] == 1
        and peaks.shape[2] == 8
        and faces.shape[0] == 8
        and faces.shape[-1] // 2 % (8 * T) == 0
        and coarse.shape[-1] // 2 % (8 * T) == 0
        and T * faces.shape[0] <= LANES
    )
    return split_body(T, NS, *args) if fits else body(*args)


def solution(mesh):
    return jax.shard_map(
        functools.partial(choose, mesh.shape["tile"], mesh.shape["sec"]),
        mesh=mesh,
        in_specs=(
            P(("sec", "tile"), None, None, None),
            P(("sec", "tile"), None),
            P(("sec", "tile")),
            P(("sec", "tile"), None, None),
            P(("sec", "tile"), None, None),
            P(("sec", "tile"), None, None),
            P(("sec", "tile"), None, None, None),
            P(("sec", "tile"), None, None, None),
            P(("sec", "tile"), None, None),
        ),
        out_specs=(
            P(("sec", "tile"), None, None),
            P(("sec", "tile"), None),
            P(("sec", "tile"), None, None),
        ),
        check_vma=False,
    )
```

```python
import functools

import jax
import jax.numpy as jnp
import ml_dtypes
import numpy as np
from jax import lax
from jax.experimental import pallas as pl
from jax.experimental.pallas import tpu as pltpu
from jax.sharding import PartitionSpec as P

TWO_PI = 6.283185307179586
LANES = 128
MESH = pl.DeviceIdType.MESH


def from_behind(value, axis, steps):
    count = lax.axis_size(axis)
    first, last = (max(0, -steps), min(count, count - steps))
    return lax.ppermute(value, axis, [(source, source + steps) for source in range(first, last)])


def window_weights(extent):
    positions = jnp.arange(extent, dtype=jnp.float32)
    return 0.5 - 0.5 * jnp.cos((positions + 0.5) * (TWO_PI / extent))


def dft_tables(extent):
    indices = jnp.arange(extent, dtype=jnp.int32)
    angles = (indices[:, None] * indices[None, :] % extent).astype(jnp.float32) * (TWO_PI / extent)
    return (jnp.cos(angles).astype(jnp.bfloat16), jnp.sin(angles).astype(jnp.bfloat16))


def spectrum(images):
    extent = images.shape[-1]
    weights = window_weights(extent)
    shaped = (images.astype(jnp.float32) * weights[:, None] * weights[None, :]).astype(jnp.bfloat16)
    cosine, sine_table = dft_tables(extent)
    segment_tables = jnp.stack([cosine, sine_table])
    segment_one = jnp.einsum(
        "jkx,...xy->...jky", segment_tables, shaped, preferred_element_type=jnp.float32
    ).astype(jnp.bfloat16)
    second_tables = jnp.stack(
        [
            jnp.concatenate([cosine, sine_table], axis=1),
            jnp.concatenate([-sine_table, cosine], axis=1),
        ]
    )
    segment_two = jnp.einsum(
        "...jky,jyl->...kl", segment_one, second_tables, preferred_element_type=jnp.float32
    )
    return (segment_two[..., :extent], -segment_two[..., extent:])


def correlate(own_spec, other_spec, peak_marks):
    own_real, own_imag = own_spec
    other_real, other_imag = other_spec
    cross_real = own_real * other_real + own_imag * other_imag
    cross_imag = own_imag * other_real - own_real * other_imag
    magnitude = jnp.sqrt(cross_real * cross_real + cross_imag * cross_imag)
    floor_value = 0.05 * jnp.mean(magnitude, axis=(-2, -1), keepdims=True) + 1e-06
    divisor = jnp.maximum(magnitude, floor_value)
    unit_real = cross_real / divisor
    unit_imag = cross_imag / divisor
    extent = own_real.shape[-1]
    indices = jnp.arange(extent, dtype=jnp.int32)
    row_angles = (peak_marks[..., 0, :, None] * indices % extent).astype(jnp.float32) * (
        TWO_PI / extent
    )
    col_angles = (peak_marks[..., 1, :, None] * indices % extent).astype(jnp.float32) * (
        TWO_PI / extent
    )
    row_cos = jnp.cos(row_angles)
    row_sin = jnp.sin(row_angles)
    high = lax.Precision.HIGHEST
    first_real = jnp.einsum("...pk,...kl->...pl", row_cos, unit_real, precision=high) - jnp.einsum(
        "...pk,...kl->...pl", row_sin, unit_imag, precision=high
    )
    first_imag = jnp.einsum("...pk,...kl->...pl", row_cos, unit_imag, precision=high) + jnp.einsum(
        "...pk,...kl->...pl", row_sin, unit_real, precision=high
    )
    return (
        jnp.sum(first_real * jnp.cos(col_angles) - first_imag * jnp.sin(col_angles), axis=-1)
        / extent
    )


def body(
    intersection_faces,
    destination,
    partner,
    face_peaks,
    coarse,
    coarse_peaks,
    upper_faces,
    lower_faces,
    section_peaks,
):
    face_dev = intersection_faces.shape[0]
    tile_dev = coarse.shape[0]
    per_tile = face_dev // tile_dev
    windows = intersection_faces.shape[1]
    peak_count = face_peaks.shape[2]
    tile_count = lax.axis_size("tile")
    capacity = max(2, (face_dev + tile_count - 1) // tile_count)
    slot_count = tile_count * capacity
    target = destination[:, 0]
    face_order = jnp.arange(face_dev, dtype=jnp.int32)
    earlier = (target[None, :] == target[:, None]) & (face_order[None, :] < face_order[:, None])
    position = jnp.sum(earlier.astype(jnp.int32), axis=1)
    slot_of = target * capacity + position
    slot_match = slot_of[None, :] == jnp.arange(slot_count, dtype=jnp.int32)[:, None]
    filled = jnp.any(slot_match, axis=1)
    source = jnp.sum(jnp.where(slot_match, face_order[None, :], 0), axis=1)
    requests = jnp.where(filled, partner[source] + 1, 0).reshape(tile_count, capacity)
    own_real, own_imag = spectrum(intersection_faces)
    parcel = jnp.einsum(
        "sf,fwxy->swxy", slot_match.astype(jnp.bfloat16), intersection_faces,
        preferred_element_type=jnp.float32,
    ).astype(jnp.bfloat16)
    parcel = parcel.reshape((tile_count, capacity) + intersection_faces.shape[1:])
    peak_marks = jnp.sum(
        jnp.where(slot_match[:, :, None, None], face_peaks[None], 0), axis=1
    ).reshape((tile_count, capacity) + face_peaks.shape[1:])
    got_faces, got_marks, wanted_ids = (
        lax.all_to_all(parcel, "tile", split_axis=0, concat_axis=0, tiled=True),
        lax.all_to_all(peak_marks, "tile", split_axis=0, concat_axis=0, tiled=True),
        lax.all_to_all(requests, "tile", split_axis=0, concat_axis=0, tiled=True),
    )

    def one_slot(packed):
        face_in, mark_in, wanted = packed
        chosen_slot = jnp.maximum(wanted - 1, 0)
        own_part = (own_real[chosen_slot], own_imag[chosen_slot])
        marks_all = mark_in[None]
        scores = correlate(spectrum(face_in), own_part, marks_all)
        return jnp.where(wanted > 0, scores, jnp.zeros_like(scores))

    slot_scores = lax.map(
        one_slot,
        (
            got_faces.reshape((slot_count,) + intersection_faces.shape[1:]),
            got_marks.reshape((slot_count,) + face_peaks.shape[1:]),
            wanted_ids.reshape(slot_count),
        ),
    )
    returned = lax.all_to_all(
        slot_scores.reshape(tile_count, capacity, windows, peak_count),
        "tile",
        split_axis=0,
        concat_axis=0,
        tiled=True,
    )
    fine_scores = returned.reshape(slot_count, windows, peak_count)[slot_of]
    coarse_real, coarse_imag = spectrum(coarse)
    wanted_tile = target * tile_dev + partner // per_tile
    shard_rows = lax.all_gather(coarse, "tile", axis=0, tiled=True)
    row_count = shard_rows.shape[0]
    def coarse_one(packed):
        tile_slot, wanted, mark_in = packed
        other_tile = lax.dynamic_index_in_dim(
            shard_rows, jnp.clip(wanted, 0, row_count - 1), keepdims=False
        )
        return correlate(
            (coarse_real[tile_slot], coarse_imag[tile_slot]), spectrum(other_tile), mark_in
        )

    coarse_scores = lax.map(coarse_one, (face_order // per_tile, wanted_tile, coarse_peaks))
    lower_in = from_behind(lower_faces, "sec", 1)
    section_marks = section_peaks[:, None]
    section_scores = correlate(spectrum(upper_faces), spectrum(lower_in), section_marks)
    return (fine_scores, coarse_scores, section_scores)


def np_tables(n):
    index = np.arange(n)
    angles = ((index[:, None] * index[None, :]) % n).astype(np.float32) * np.float32(TWO_PI / n)
    return np.cos(angles), np.sin(angles)


def split_tables(n, parts):
    cosine, sine = np_tables(n)
    rows = n // 2 // parts
    slots = sine[: n // 2].copy()
    slots[0] = cosine[n // 2]
    first = np.concatenate(
        [cosine[: n // 2].reshape(parts, rows, n), slots.reshape(parts, rows, n)], axis=1
    ).reshape(n, n)
    second = np.concatenate([cosine, sine], axis=1)
    marks = np.zeros((parts, 2, n, 2 * (rows + 8)), np.float32)
    for part in range(parts):
        bins = list(range(part * rows, (part + 1) * rows))
        weight = np.array([1.0 if k == 0 else 2.0 for k in bins] + [1.0 if part == 0 else 0.0] + [0.0] * 7)
        bins = bins + [n // 2] * 8
        c, s = cosine[bins].T * weight, sine[bins].T * weight
        marks[part, 0] = np.concatenate([c, -s], axis=1)
        marks[part, 1] = np.concatenate([s, c], axis=1)
    return [bf16(first), bf16(second), bf16(marks)]


def whole_tables(n):
    cosine, sine = np_tables(n)
    rows = n // 2 + 8
    first = np.concatenate([cosine[:rows], sine[:rows]], axis=0)
    weight = np.array([1.0] + [2.0] * (n // 2 - 1) + [1.0] + [0.0] * 7)
    c, s = cosine[:rows].T * weight, sine[:rows].T * weight
    marks = np.stack([np.concatenate([c, -s], axis=1), np.concatenate([s, c], axis=1)])
    return [bf16(first), bf16(marks), np.tile(weight[:, None], (1, n)).astype(np.float32)]


def bf16(table):
    return table.astype(np.float32).astype(ml_dtypes.bfloat16)


def hann(n):
    x = np.arange(n, dtype=np.float32)
    values = (0.5 - 0.5 * np.cos((x + np.float32(0.5)) * np.float32(TWO_PI / n))).astype(np.float32)
    return [values[:, None], values[None, :]]


def iota(shape, axis):
    return lax.broadcasted_iota(jnp.int32, shape, axis)


def mm(a, b):
    return jnp.dot(a, b, preferred_element_type=jnp.float32)


def pick(onehot, table):
    return lax.dot_general(
        onehot, table, (((0,), (0,)), ((), ())), preferred_element_type=jnp.float32
    )


def fold(value):
    total = value[:, :LANES]
    for start in range(LANES, value.shape[1], LANES):
        total = total + value[:, start : start + LANES]
    return total


def windowed(image, column, row):
    return (image.astype(jnp.float32) * column * row).astype(jnp.bfloat16)


def cross(ar, ai, br, bi):
    xr = ar * br + ai * bi
    xi = ai * br - ar * bi
    power = xr * xr + xi * xi
    inverse = lax.rsqrt(jnp.maximum(power, 1e-37))
    return xr, xi, inverse, power * inverse


def to_row(column, shift):
    shape = (column.shape[0], LANES)
    here = iota(shape, 1) == iota(shape, 0) + shift
    return jnp.sum(jnp.where(here, column, 0.0), axis=0, keepdims=True)


def to_grid(rows, shift, count):
    shape = (8, LANES)
    kept = jnp.where(iota(shape, 1) // count == iota(shape, 0) + shift, rows, 0.0)
    chosen = (iota((LANES, count), 0) % count == iota((LANES, count), 1)).astype(jnp.float32)
    return jnp.dot(kept, chosen, precision=lax.Precision.HIGHEST, preferred_element_type=jnp.float32)


def kernel(
    T, NS, h_dest, h_part, h_fp, h_cp, h_sp, h_faces, h_coarse, h_upper, lower,
    h_f_col, h_f_row, h_c_col, h_c_row, h_f_first, h_f_second, h_f_marks,
    h_c_first, h_c_second, h_c_marks, h_s_first, h_s_marks, h_s_weight,
    fine_out, coarse_out, section_out,
    dest, part, fp, cp, sp, faces, coarse, upper, f_col, f_row, c_col, c_row,
    f_first, f_second, f_marks, c_first, c_second, c_marks, s_first, s_marks, s_weight,
    load_sems, ints, ints_all, ints_sm, low, f_send, f_all, c_send, c_all,
    f_sr, f_si, c_sr, c_si, f_xr, f_xi, f_in, c_xr, c_xi, c_in,
    f_a, f_cs, c_a, c_cs, f_sums, c_sums, f_msg, c_msg, f_tot, c_tot, f_it, c_it,
    f_part, c_part, out_msg, out_all,
    send_sems, recv_sems, low_sems, local_sem,
):
    me, sec = lax.axis_index("tile"), lax.axis_index("sec")
    loads = [
        pltpu.make_async_copy(source, target, load_sems.at[index])
        for index, (source, target) in enumerate([
            (h_f_col, f_col), (h_f_row, f_row), (h_f_first, f_first), (h_faces, faces),
            (h_dest, dest), (h_part, part), (h_fp, fp), (h_cp, cp), (h_sp, sp),
            (h_c_col, c_col), (h_c_row, c_row), (h_c_first, c_first), (h_coarse, coarse),
            (h_f_second, f_second), (h_f_marks.at[me], f_marks),
            (h_c_second, c_second), (h_c_marks.at[me], c_marks),
            (h_upper, upper), (h_s_first, s_first), (h_s_marks, s_marks), (h_s_weight, s_weight),
        ])
    ]
    for load in loads:
        load.start()

    def loaded(low_at, high_at):
        for load in loads[low_at:high_at]:
            load.wait()

    FD, TD = faces.shape[0], coarse.shape[0]
    per_tile = FD // TD
    PK = fine_out.shape[1]
    pairs = T * FD
    barrier = pltpu.get_barrier_semaphore()
    for step in range(1, T):
        pl.semaphore_signal(barrier, inc=1, device_id={"tile": lax.rem(me + step, T)}, device_id_type=MESH)

    @pl.when(sec < NS - 1)
    def _():
        pl.semaphore_signal(barrier, inc=1, device_id={"sec": sec + 1}, device_id_type=MESH)

    @pl.when(sec > 0)
    def _():
        pl.semaphore_signal(barrier, inc=1, device_id={"sec": sec - 1}, device_id_type=MESH)

    def exchange(kind, step, source, landing):
        peer = lax.rem(me + step, T)
        return pltpu.make_async_remote_copy(
            src_ref=source(peer), dst_ref=landing.at[me], send_sem=send_sems.at[kind, step],
            recv_sem=recv_sems.at[kind, me], device_id={"tile": peer}, device_id_type=MESH,
        )

    def start(kind, source, landing):
        for step in range(1, T):
            exchange(kind, step, source, landing).start()

    def arrive(kind, source, landing):
        for step in range(1, T):
            peer = lax.rem(me + step, T)
            pltpu.make_async_remote_copy(
                src_ref=source(peer), dst_ref=landing.at[peer], send_sem=send_sems.at[kind, step],
                recv_sem=recv_sems.at[kind, peer], device_id={"tile": peer}, device_id_type=MESH,
            ).wait_recv()

    def sent(kind, source, landing):
        for step in range(1, T):
            exchange(kind, step, source, landing).wait_send()

    def lower_copy():
        return pltpu.make_async_remote_copy(
            src_ref=lower, dst_ref=low, send_sem=low_sems.at[0], recv_sem=low_sems.at[1],
            device_id={"sec": lax.rem(sec + 1, NS)}, device_id_type=MESH,
        )

    def first_step(images, col, row, table, out, count):
        n = images.shape[-1]
        for which in range(count):
            got = mm(table[...], windowed(images[which], col[...], row[...]))
            out[:, which] = got.astype(jnp.bfloat16).reshape(T, n // T, n)

    def lanes_of(grid, shift):
        count, width = grid.shape
        chosen = iota((width, LANES), 1) % width == iota((width, LANES), 0)
        spread = mm(grid.astype(jnp.float32).astype(jnp.bfloat16), chosen.astype(jnp.float32).astype(jnp.bfloat16))
        shape = (count, LANES)
        kept = iota(shape, 1) // width == iota(shape, 0) + shift
        return jnp.sum(jnp.where(kept, spread, 0.0), axis=0, keepdims=True)

    loaded(4, 9)
    lines = [
        lanes_of(fp[:, 0, :], 0) + lanes_of(fp[:, 1, :], FD),
        lanes_of(cp[:, 0, :], 0) + lanes_of(cp[:, 1, :], FD),
        lanes_of(sp[:, 0, :], 0) + lanes_of(sp[:, 1, :], TD),
    ]
    lines = jnp.concatenate(lines + [jnp.zeros((5, LANES), jnp.float32)], axis=0)
    ints[...] = (lines + 0.5).astype(jnp.int32)
    ints[3:4, :FD] = dest[...]
    ints[4:5, :FD] = part[...]
    loaded(0, 4)
    first_step(faces, f_col, f_row, f_first, f_send, FD)

    @pl.when((sec > 0) & (sec < NS - 1))
    def _():
        pl.semaphore_wait(barrier, T + 1)

    @pl.when((sec == 0) | (sec == NS - 1))
    def _():
        pl.semaphore_wait(barrier, T - 1 + (1 if NS > 1 else 0))

    sources = [lambda peer: ints, lambda peer: f_send.at[peer], lambda peer: c_send.at[peer],
               lambda peer: f_msg, lambda peer: c_msg, lambda peer: out_msg.at[peer]]
    landings = [ints_all, f_all, c_all, f_tot, c_tot, out_all]
    start(0, sources[0], landings[0])
    start(1, sources[1], landings[1])

    @pl.when(sec < NS - 1)
    def _():
        lower_copy().start()

    loaded(9, 13)
    first_step(coarse, c_col, c_row, c_first, c_send, TD)
    start(2, sources[2], landings[2])
    ints_all[me] = ints[...]
    f_all[me] = f_send[me]
    c_all[me] = c_send[me]

    loaded(13, len(loads))
    arrive(0, sources[0], landings[0])
    to_scalar = pltpu.make_async_copy(ints_all, ints_sm, local_sem)
    to_scalar.start()

    def tables_of(row, n, second, marks, a, cs, at):
        onehot = jnp.where(iota((n, LANES), 0) == row, 1.0, 0.0).astype(jnp.bfloat16)
        half = FD * PK
        width = 2 * n
        cs[pl.ds(at, FD)] = pick(onehot, second)[half:].reshape(FD, PK, width)
        for side in range(2):
            a[pl.ds(at, FD), side * PK : (side + 1) * PK, :] = pick(onehot, marks[side])[:half].reshape(FD, PK, -1)

    def peaks_from(j, _):
        rows = ints_all[j]
        tables_of(rows[0:1], f_row.shape[1], f_second[...], f_marks, f_a, f_cs, j * FD)
        tables_of(rows[1:2], c_row.shape[1], c_second[...], c_marks, c_a, c_cs, j * FD)
        return 0

    lax.fori_loop(0, T, peaks_from, 0, unroll=4)

    @pl.when(sec > 0)
    def _():
        lower_copy().wait_recv()

    @pl.when(sec == 0)
    def _():
        low[...] = jnp.zeros_like(low)

    n = f_row.shape[1]
    rows_s = n // 2 + 8

    def spectrum_s(image):
        got = mm(s_first[...], windowed(image, f_col[...], f_row[...])).astype(jnp.bfloat16)
        both = mm(got, f_second[...])
        p, q = both[:rows_s], both[rows_s:]
        return p[:, :n] - q[:, n:], -(p[:, n:] + q[:, :n])

    onehot = jnp.where(iota((n, LANES), 0) == ints[2:3], 1.0, 0.0).astype(jnp.bfloat16)
    cs_s = pick(onehot, f_second[...])[TD * PK : 2 * TD * PK]
    a_s = [pick(onehot, s_marks[side])[: TD * PK] for side in range(2)]
    columns = []
    for which in range(TD):
        ar, ai = spectrum_s(upper[which])
        br, bi = spectrum_s(low[which])
        xr, xi, inverse, size = cross(ar, ai, br, bi)
        total = jnp.sum(jnp.sum(size * s_weight[...], axis=0, keepdims=True), axis=1, keepdims=True)
        scale = jnp.minimum(inverse, 1.0 / (total * (0.05 / (n * n)) + 1e-6))
        unit = jnp.concatenate([xr * scale, xi * scale], axis=0).astype(jnp.bfloat16)
        at = slice(which * PK, (which + 1) * PK)
        fr = mm(a_s[0][at].astype(jnp.bfloat16), unit)
        fi = mm(a_s[1][at].astype(jnp.bfloat16), unit)
        columns.append(jnp.sum(fr * cs_s[at, :n] - fi * cs_s[at, n:], axis=1, keepdims=True))
    row = to_row(jnp.concatenate(columns, axis=0), 0)
    section_out[...] = to_grid(jnp.broadcast_to(row, (8, LANES)), 0, PK)[:TD] * (1.0 / n)

    to_scalar.wait()

    def second_step(block, n, second, sr, si, groups):
        rows = n // 2 // T
        per = T // groups
        images = block.shape[1]
        for group in range(groups):
            x = block[group * per : (group + 1) * per].reshape(per * images * 2 * rows, n)
            both = mm(x, second[...]).reshape(per * images, 2 * rows, 2 * n)
            p, q = both[:, :rows], both[:, rows:]
            special = (iota((1, rows, 1), 1) == 0) & (me == 0)
            at = slice(group * per * images, (group + 1) * per * images)
            sr[at, :rows, :] = p[:, :, :n] - jnp.where(special, 0.0, q[:, :, n:])
            si[at, :rows, :] = -(p[:, :, n:] + jnp.where(special, 0.0, q[:, :, :n]))
            sr[at, rows:, :] = q[:, :8, :n]
            si[at, rows:, :] = -q[:, :8, n:]

    def weights(rows, n):
        at = iota((rows + 8, n), 0)
        main = jnp.where((at == 0) & (me == 0), 1.0, 2.0)
        extra = jnp.where((at == rows) & (me == 0), 1.0, 0.0)
        return jnp.where(at < rows, main, extra)

    def cross_all(n, sr, si, xr, xi, inv, sums, own_of, other_of, msg):
        w = weights(n // 2 // T, n)

        def one(p, _):
            own, other = own_of(p), other_of(p)
            vr, vi, inverse, size = cross(sr[own], si[own], sr[other], si[other])
            xr[p], xi[p], inv[p] = vr, vi, inverse
            sums[pl.ds(p, 1), :] = fold(jnp.sum(size * w, axis=0, keepdims=True))
            return 0

        lax.fori_loop(0, pairs, one, 0, unroll=8)
        total = jnp.sum(sums[...], axis=1, keepdims=True)
        msg[...] = jnp.broadcast_to(to_row(total, 0), msg.shape)

    def score_all(n, tot, it, xr, xi, inv, a, cs, part):
        row = jnp.sum(tot[...], axis=0)[0:1]
        limit = 1.0 / (row * (0.05 / (n * n)) + 1e-6)
        shape = (pairs, LANES)
        column = jnp.sum(jnp.where(iota(shape, 1) == iota(shape, 0), limit, 0.0), axis=1, keepdims=True)
        it[...] = jnp.broadcast_to(column, it.shape)

        def one(p, _):
            scale = jnp.minimum(inv[p], it[pl.ds(p, 1), :])
            unit = jnp.concatenate([xr[p] * scale, xi[p] * scale], axis=0).astype(jnp.bfloat16)
            got = mm(a[p].astype(jnp.bfloat16), unit)
            table = cs[p]
            part[p] = fold(got[:PK] * table[:, :n] - got[PK:] * table[:, n:])
            return 0

        lax.fori_loop(0, pairs, one, 0, unroll=16)

    NF, NC = f_row.shape[1], c_row.shape[1]
    arrive(1, sources[1], landings[1])
    second_step(f_all, NF, f_second, f_sr, f_si, 2)
    cross_all(
        NF, f_sr, f_si, f_xr, f_xi, f_in, f_sums, lambda p: p,
        lambda p: jnp.clip(ints_sm[p // FD, 3, p % FD] * FD + ints_sm[p // FD, 4, p % FD], 0, pairs - 1), f_msg,
    )
    start(3, sources[3], landings[3])
    f_tot[me] = f_msg[...]
    arrive(2, sources[2], landings[2])
    second_step(c_all, NC, c_second, c_sr, c_si, 2)
    cross_all(
        NC, c_sr, c_si, c_xr, c_xi, c_in, c_sums, lambda p: p // per_tile,
        lambda p: jnp.clip(ints_sm[p // FD, 3, p % FD] * TD + ints_sm[p // FD, 4, p % FD] // per_tile, 0, T * TD - 1), c_msg,
    )
    start(4, sources[4], landings[4])
    c_tot[me] = c_msg[...]
    arrive(3, sources[3], landings[3])
    score_all(NF, f_tot, f_it, f_xr, f_xi, f_in, f_a, f_cs, f_part)
    arrive(4, sources[4], landings[4])
    score_all(NC, c_tot, c_it, c_xr, c_xi, c_in, c_a, c_cs, c_part)

    def gather(j, _):
        def column(part):
            block = part[pl.ds(j * FD, FD)].reshape(FD * PK, LANES)
            return jnp.sum(block, axis=1, keepdims=True)

        row = to_row(column(c_part), 0) + to_row(column(f_part), FD * PK)
        out_msg[j] = jnp.broadcast_to(row, (8, LANES))
        return 0

    lax.fori_loop(0, T, gather, 0, unroll=8)
    start(5, sources[5], landings[5])
    out_all[me] = out_msg[me]
    for kind in range(5):
        sent(kind, sources[kind], landings[kind])

    @pl.when(sec < NS - 1)
    def _():
        lower_copy().wait_send()

    arrive(5, sources[5], landings[5])
    total = jnp.sum(out_all[...], axis=0)
    coarse_out[...] = to_grid(total, 0, PK) * (1.0 / NC)
    fine_out[...] = to_grid(total, FD, PK) * (1.0 / NF)
    sent(5, sources[5], landings[5])


def split_body(
    T, NS, intersection_faces, destination, partner, face_peaks, coarse, coarse_peaks,
    upper_faces, lower_faces, section_peaks,
):
    FD, TD, PK = intersection_faces.shape[0], coarse.shape[0], face_peaks.shape[2]
    NF, NC = intersection_faces.shape[-1], coarse.shape[-1]
    pairs = T * FD

    operands = [
        destination.reshape(1, FD), partner.reshape(1, FD), face_peaks, coarse_peaks, section_peaks,
        intersection_faces.reshape(FD, NF, NF), coarse,
        upper_faces.reshape(TD, NF, NF), lower_faces.reshape(TD, NF, NF),
    ] + [jnp.asarray(t) for t in (
        hann(NF) + hann(NC) + split_tables(NF, T) + split_tables(NC, T) + whole_tables(NF)
    )]
    fr, cr = NF // 2 // T + 8, NC // 2 // T + 8
    f32 = jnp.float32
    V = pltpu.VMEM
    kept = [(x.shape[1:] if x.ndim == 4 else x.shape, x.dtype) for x in operands]
    scratch = [V(*one) for index, one in enumerate(kept) if index != 8] + [
        pltpu.SemaphoreType.DMA((len(operands) - 1,)), V((8, LANES), jnp.int32),
        V((T, 8, LANES), jnp.int32), pltpu.SMEM((T, 8, LANES), jnp.int32),
        V((TD, NF, NF), jnp.bfloat16),
        V((T, FD, NF // T, NF), jnp.bfloat16), V((T, FD, NF // T, NF), jnp.bfloat16),
        V((T, TD, NC // T, NC), jnp.bfloat16), V((T, TD, NC // T, NC), jnp.bfloat16),
        V((pairs, fr, NF), f32), V((pairs, fr, NF), f32),
        V((T * TD, cr, NC), f32), V((T * TD, cr, NC), f32),
    ] + [V((pairs, fr, NF), f32)] * 3 + [V((pairs, cr, NC), f32)] * 3 + [
        V((pairs, 2 * PK, 2 * fr), f32), V((pairs, PK, 2 * NF), f32),
        V((pairs, 2 * PK, 2 * cr), f32), V((pairs, PK, 2 * NC), f32),
        V((pairs, LANES), f32), V((pairs, LANES), f32),
        V((8, LANES), f32), V((8, LANES), f32),
        V((T, 8, LANES), f32), V((T, 8, LANES), f32),
        V((pairs, NF), f32), V((pairs, NC), f32),
        V((pairs, PK, LANES), f32), V((pairs, PK, LANES), f32),
        V((T, 8, LANES), f32), V((T, 8, LANES), f32),
        pltpu.SemaphoreType.DMA((6, T)), pltpu.SemaphoreType.DMA((6, T)),
        pltpu.SemaphoreType.DMA((2,)), pltpu.SemaphoreType.DMA,
    ]
    fine, coarse_scores, section = pl.pallas_call(
        functools.partial(kernel, T, NS),
        out_shape=(
            jax.ShapeDtypeStruct((FD, PK), f32), jax.ShapeDtypeStruct((FD, PK), f32),
            jax.ShapeDtypeStruct((TD, PK), f32),
        ),
        in_specs=[pl.BlockSpec(memory_space=pltpu.HBM)] * len(operands),
        out_specs=(pl.BlockSpec(memory_space=pltpu.VMEM),) * 3,
        scratch_shapes=scratch,
        compiler_params=pltpu.CompilerParams(
            collective_id=0, has_side_effects=True, vmem_limit_bytes=60 * 1024 * 1024
        ),
    )(*operands)
    return fine.reshape(FD, 1, PK), coarse_scores, section.reshape(TD, 1, PK)


def choose(T, NS, *args):
    faces, coarse, peaks = args[0], args[4], args[3]
    fits = (
        faces.shape[1] == 1
        and peaks.shape[2] == 8
        and faces.shape[0] == 8
        and faces.shape[-1] // 2 % (8 * T) == 0
        and coarse.shape[-1] // 2 % (8 * T) == 0
        and T * faces.shape[0] <= LANES
    )
    return split_body(T, NS, *args) if fits else body(*args)


def solution(mesh):
    return jax.shard_map(
        functools.partial(choose, mesh.shape["tile"], mesh.shape["sec"]),
        mesh=mesh,
        in_specs=(
            P(("sec", "tile"), None, None, None),
            P(("sec", "tile"), None),
            P(("sec", "tile")),
            P(("sec", "tile"), None, None),
            P(("sec", "tile"), None, None),
            P(("sec", "tile"), None, None),
            P(("sec", "tile"), None, None, None),
            P(("sec", "tile"), None, None, None),
            P(("sec", "tile"), None, None),
        ),
        out_specs=(
            P(("sec", "tile"), None, None),
            P(("sec", "tile"), None),
            P(("sec", "tile"), None, None),
        ),
        check_vma=False,
    )
```

```python
import functools

import jax
import jax.numpy as jnp
import ml_dtypes
import numpy as np
from jax import lax
from jax.experimental import pallas as pl
from jax.experimental.pallas import tpu as pltpu
from jax.sharding import PartitionSpec as P

TWO_PI = 6.283185307179586
LANES = 128
MESH = pl.DeviceIdType.MESH


def from_behind(value, axis, steps):
    count = lax.axis_size(axis)
    first, last = (max(0, -steps), min(count, count - steps))
    return lax.ppermute(value, axis, [(source, source + steps) for source in range(first, last)])


def window_weights(extent):
    positions = jnp.arange(extent, dtype=jnp.float32)
    return 0.5 - 0.5 * jnp.cos((positions + 0.5) * (TWO_PI / extent))


def dft_tables(extent):
    indices = jnp.arange(extent, dtype=jnp.int32)
    angles = (indices[:, None] * indices[None, :] % extent).astype(jnp.float32) * (TWO_PI / extent)
    return (jnp.cos(angles).astype(jnp.bfloat16), jnp.sin(angles).astype(jnp.bfloat16))


def spectrum(images):
    extent = images.shape[-1]
    weights = window_weights(extent)
    shaped = (images.astype(jnp.float32) * weights[:, None] * weights[None, :]).astype(jnp.bfloat16)
    cosine, sine_table = dft_tables(extent)
    segment_tables = jnp.stack([cosine, sine_table])
    segment_one = jnp.einsum(
        "jkx,...xy->...jky", segment_tables, shaped, preferred_element_type=jnp.float32
    ).astype(jnp.bfloat16)
    second_tables = jnp.stack(
        [
            jnp.concatenate([cosine, sine_table], axis=1),
            jnp.concatenate([-sine_table, cosine], axis=1),
        ]
    )
    segment_two = jnp.einsum(
        "...jky,jyl->...kl", segment_one, second_tables, preferred_element_type=jnp.float32
    )
    return (segment_two[..., :extent], -segment_two[..., extent:])


def correlate(own_spec, other_spec, peak_marks):
    own_real, own_imag = own_spec
    other_real, other_imag = other_spec
    cross_real = own_real * other_real + own_imag * other_imag
    cross_imag = own_imag * other_real - own_real * other_imag
    magnitude = jnp.sqrt(cross_real * cross_real + cross_imag * cross_imag)
    floor_value = 0.05 * jnp.mean(magnitude, axis=(-2, -1), keepdims=True) + 1e-06
    divisor = jnp.maximum(magnitude, floor_value)
    unit_real = cross_real / divisor
    unit_imag = cross_imag / divisor
    extent = own_real.shape[-1]
    indices = jnp.arange(extent, dtype=jnp.int32)
    row_angles = (peak_marks[..., 0, :, None] * indices % extent).astype(jnp.float32) * (
        TWO_PI / extent
    )
    col_angles = (peak_marks[..., 1, :, None] * indices % extent).astype(jnp.float32) * (
        TWO_PI / extent
    )
    row_cos = jnp.cos(row_angles)
    row_sin = jnp.sin(row_angles)
    high = lax.Precision.HIGHEST
    first_real = jnp.einsum("...pk,...kl->...pl", row_cos, unit_real, precision=high) - jnp.einsum(
        "...pk,...kl->...pl", row_sin, unit_imag, precision=high
    )
    first_imag = jnp.einsum("...pk,...kl->...pl", row_cos, unit_imag, precision=high) + jnp.einsum(
        "...pk,...kl->...pl", row_sin, unit_real, precision=high
    )
    return (
        jnp.sum(first_real * jnp.cos(col_angles) - first_imag * jnp.sin(col_angles), axis=-1)
        / extent
    )


def body(
    intersection_faces,
    destination,
    partner,
    face_peaks,
    coarse,
    coarse_peaks,
    upper_faces,
    lower_faces,
    section_peaks,
):
    face_dev = intersection_faces.shape[0]
    tile_dev = coarse.shape[0]
    per_tile = face_dev // tile_dev
    windows = intersection_faces.shape[1]
    peak_count = face_peaks.shape[2]
    tile_count = lax.axis_size("tile")
    capacity = max(2, (face_dev + tile_count - 1) // tile_count)
    slot_count = tile_count * capacity
    target = destination[:, 0]
    face_order = jnp.arange(face_dev, dtype=jnp.int32)
    earlier = (target[None, :] == target[:, None]) & (face_order[None, :] < face_order[:, None])
    position = jnp.sum(earlier.astype(jnp.int32), axis=1)
    slot_of = target * capacity + position
    slot_match = slot_of[None, :] == jnp.arange(slot_count, dtype=jnp.int32)[:, None]
    filled = jnp.any(slot_match, axis=1)
    source = jnp.sum(jnp.where(slot_match, face_order[None, :], 0), axis=1)
    requests = jnp.where(filled, partner[source] + 1, 0).reshape(tile_count, capacity)
    own_real, own_imag = spectrum(intersection_faces)
    parcel = jnp.einsum(
        "sf,fwxy->swxy", slot_match.astype(jnp.bfloat16), intersection_faces,
        preferred_element_type=jnp.float32,
    ).astype(jnp.bfloat16)
    parcel = parcel.reshape((tile_count, capacity) + intersection_faces.shape[1:])
    peak_marks = jnp.sum(
        jnp.where(slot_match[:, :, None, None], face_peaks[None], 0), axis=1
    ).reshape((tile_count, capacity) + face_peaks.shape[1:])
    got_faces, got_marks, wanted_ids = (
        lax.all_to_all(parcel, "tile", split_axis=0, concat_axis=0, tiled=True),
        lax.all_to_all(peak_marks, "tile", split_axis=0, concat_axis=0, tiled=True),
        lax.all_to_all(requests, "tile", split_axis=0, concat_axis=0, tiled=True),
    )

    def one_slot(packed):
        face_in, mark_in, wanted = packed
        chosen_slot = jnp.maximum(wanted - 1, 0)
        own_part = (own_real[chosen_slot], own_imag[chosen_slot])
        marks_all = mark_in[None]
        scores = correlate(spectrum(face_in), own_part, marks_all)
        return jnp.where(wanted > 0, scores, jnp.zeros_like(scores))

    slot_scores = lax.map(
        one_slot,
        (
            got_faces.reshape((slot_count,) + intersection_faces.shape[1:]),
            got_marks.reshape((slot_count,) + face_peaks.shape[1:]),
            wanted_ids.reshape(slot_count),
        ),
    )
    returned = lax.all_to_all(
        slot_scores.reshape(tile_count, capacity, windows, peak_count),
        "tile",
        split_axis=0,
        concat_axis=0,
        tiled=True,
    )
    fine_scores = returned.reshape(slot_count, windows, peak_count)[slot_of]
    coarse_real, coarse_imag = spectrum(coarse)
    wanted_tile = target * tile_dev + partner // per_tile
    shard_rows = lax.all_gather(coarse, "tile", axis=0, tiled=True)
    row_count = shard_rows.shape[0]
    def coarse_one(packed):
        tile_slot, wanted, mark_in = packed
        other_tile = lax.dynamic_index_in_dim(
            shard_rows, jnp.clip(wanted, 0, row_count - 1), keepdims=False
        )
        return correlate(
            (coarse_real[tile_slot], coarse_imag[tile_slot]), spectrum(other_tile), mark_in
        )

    coarse_scores = lax.map(coarse_one, (face_order // per_tile, wanted_tile, coarse_peaks))
    lower_in = from_behind(lower_faces, "sec", 1)
    section_marks = section_peaks[:, None]
    section_scores = correlate(spectrum(upper_faces), spectrum(lower_in), section_marks)
    return (fine_scores, coarse_scores, section_scores)


def np_tables(n):
    index = np.arange(n)
    angles = ((index[:, None] * index[None, :]) % n).astype(np.float32) * np.float32(TWO_PI / n)
    return np.cos(angles), np.sin(angles)


def split_tables(n, parts):
    cosine, sine = np_tables(n)
    rows = n // 2 // parts
    slots = sine[: n // 2].copy()
    slots[0] = cosine[n // 2]
    first = np.concatenate(
        [cosine[: n // 2].reshape(parts, rows, n), slots.reshape(parts, rows, n)], axis=1
    ).reshape(n, n)
    second = np.concatenate([cosine, sine], axis=1)
    marks = np.zeros((parts, 2, n, 2 * (rows + 8)), np.float32)
    for part in range(parts):
        bins = list(range(part * rows, (part + 1) * rows))
        weight = np.array([1.0 if k == 0 else 2.0 for k in bins] + [1.0 if part == 0 else 0.0] + [0.0] * 7)
        bins = bins + [n // 2] * 8
        c, s = cosine[bins].T * weight, sine[bins].T * weight
        marks[part, 0] = np.concatenate([c, -s], axis=1)
        marks[part, 1] = np.concatenate([s, c], axis=1)
    return [bf16(first), bf16(second), bf16(marks)]


def whole_tables(n):
    cosine, sine = np_tables(n)
    rows = n // 2 + 8
    first = np.concatenate([cosine[:rows], sine[:rows]], axis=0)
    weight = np.array([1.0] + [2.0] * (n // 2 - 1) + [1.0] + [0.0] * 7)
    c, s = cosine[:rows].T * weight, sine[:rows].T * weight
    marks = np.stack([np.concatenate([c, -s], axis=1), np.concatenate([s, c], axis=1)])
    return [bf16(first), bf16(marks), np.tile(weight[:, None], (1, n)).astype(np.float32)]


def bf16(table):
    return table.astype(np.float32).astype(ml_dtypes.bfloat16)


def hann(n):
    x = np.arange(n, dtype=np.float32)
    values = (0.5 - 0.5 * np.cos((x + np.float32(0.5)) * np.float32(TWO_PI / n))).astype(np.float32)
    return [values[:, None], values[None, :]]


def iota(shape, axis):
    return lax.broadcasted_iota(jnp.int32, shape, axis)


def mm(a, b):
    return jnp.dot(a, b, preferred_element_type=jnp.float32)


def pick(onehot, table):
    return lax.dot_general(
        onehot, table, (((0,), (0,)), ((), ())), preferred_element_type=jnp.float32
    )


def fold(value):
    total = value[:, :LANES]
    for start in range(LANES, value.shape[1], LANES):
        total = total + value[:, start : start + LANES]
    return total


def windowed(image, column, row):
    return (image.astype(jnp.float32) * column * row).astype(jnp.bfloat16)


def cross(ar, ai, br, bi):
    xr = ar * br + ai * bi
    xi = ai * br - ar * bi
    power = xr * xr + xi * xi
    inverse = lax.rsqrt(jnp.maximum(power, 1e-37))
    return xr, xi, inverse, power * inverse


def to_row(column, shift):
    shape = (column.shape[0], LANES)
    here = iota(shape, 1) == iota(shape, 0) + shift
    return jnp.sum(jnp.where(here, column, 0.0), axis=0, keepdims=True)


def to_grid(rows, shift, count):
    shape = (8, LANES)
    kept = jnp.where(iota(shape, 1) // count == iota(shape, 0) + shift, rows, 0.0)
    chosen = (iota((LANES, count), 0) % count == iota((LANES, count), 1)).astype(jnp.float32)
    return jnp.dot(kept, chosen, precision=lax.Precision.HIGHEST, preferred_element_type=jnp.float32)


def kernel(
    T, NS, h_dest, h_part, h_fp, h_cp, h_sp, h_faces, h_coarse, h_upper, lower,
    h_f_col, h_f_row, h_c_col, h_c_row, h_f_first, h_f_second, h_f_marks,
    h_c_first, h_c_second, h_c_marks, h_s_first, h_s_marks, h_s_weight,
    fine_out, coarse_out, section_out,
    dest, part, fp, cp, sp, faces, coarse, upper, f_col, f_row, c_col, c_row,
    f_first, f_second, f_marks, c_first, c_second, c_marks, s_first, s_marks, s_weight,
    load_sems, ints, ints_all, ints_sm, low, f_send, f_all, c_send, c_all,
    f_sr, f_si, c_sr, c_si, f_xr, f_xi, f_in, c_xr, c_xi, c_in,
    f_a, f_cs, c_a, c_cs, f_sums, c_sums, f_msg, c_msg, f_tot, c_tot, f_it, c_it,
    f_part, c_part, out_msg, out_all,
    send_sems, recv_sems, low_sems, local_sem,
):
    me, sec = lax.axis_index("tile"), lax.axis_index("sec")
    loads = [
        pltpu.make_async_copy(source, target, load_sems.at[index])
        for index, (source, target) in enumerate([
            (h_f_col, f_col), (h_f_row, f_row), (h_f_first, f_first), (h_faces, faces),
            (h_dest, dest), (h_part, part), (h_fp, fp), (h_cp, cp), (h_sp, sp),
            (h_c_col, c_col), (h_c_row, c_row), (h_c_first, c_first), (h_coarse, coarse),
            (h_f_second, f_second), (h_f_marks.at[me], f_marks),
            (h_c_second, c_second), (h_c_marks.at[me], c_marks),
            (h_upper, upper), (h_s_first, s_first), (h_s_marks, s_marks), (h_s_weight, s_weight),
        ])
    ]
    for load in loads:
        load.start()

    def loaded(low_at, high_at):
        for load in loads[low_at:high_at]:
            load.wait()

    FD, TD = faces.shape[0], coarse.shape[0]
    per_tile = FD // TD
    PK = fine_out.shape[1]
    pairs = T * FD
    barrier = pltpu.get_barrier_semaphore()
    for step in range(1, T):
        pl.semaphore_signal(barrier, inc=1, device_id={"tile": lax.rem(me + step, T)}, device_id_type=MESH)

    @pl.when(sec < NS - 1)
    def _():
        pl.semaphore_signal(barrier, inc=1, device_id={"sec": sec + 1}, device_id_type=MESH)

    @pl.when(sec > 0)
    def _():
        pl.semaphore_signal(barrier, inc=1, device_id={"sec": sec - 1}, device_id_type=MESH)

    def exchange(kind, step, source, landing):
        peer = lax.rem(me + step, T)
        return pltpu.make_async_remote_copy(
            src_ref=source(peer), dst_ref=landing.at[me], send_sem=send_sems.at[kind, step],
            recv_sem=recv_sems.at[kind, me], device_id={"tile": peer}, device_id_type=MESH,
        )

    def start(kind, source, landing):
        for step in range(1, T):
            exchange(kind, step, source, landing).start()

    def arrive(kind, source, landing):
        for step in range(1, T):
            peer = lax.rem(me + step, T)
            pltpu.make_async_remote_copy(
                src_ref=source(peer), dst_ref=landing.at[peer], send_sem=send_sems.at[kind, step],
                recv_sem=recv_sems.at[kind, peer], device_id={"tile": peer}, device_id_type=MESH,
            ).wait_recv()

    def sent(kind, source, landing):
        for step in range(1, T):
            exchange(kind, step, source, landing).wait_send()

    def lower_copy():
        return pltpu.make_async_remote_copy(
            src_ref=lower, dst_ref=low, send_sem=low_sems.at[0], recv_sem=low_sems.at[1],
            device_id={"sec": lax.rem(sec + 1, NS)}, device_id_type=MESH,
        )

    def first_step(images, col, row, table, out, count):
        n = images.shape[-1]
        for which in range(count):
            got = mm(table[...], windowed(images[which], col[...], row[...]))
            out[:, which] = got.astype(jnp.bfloat16).reshape(T, n // T, n)

    def lanes_of(grid, shift):
        count, width = grid.shape
        chosen = iota((width, LANES), 1) % width == iota((width, LANES), 0)
        spread = mm(grid.astype(jnp.float32).astype(jnp.bfloat16), chosen.astype(jnp.float32).astype(jnp.bfloat16))
        shape = (count, LANES)
        kept = iota(shape, 1) // width == iota(shape, 0) + shift
        return jnp.sum(jnp.where(kept, spread, 0.0), axis=0, keepdims=True)

    loaded(4, 9)
    lines = [
        lanes_of(fp[:, 0, :], 0) + lanes_of(fp[:, 1, :], FD),
        lanes_of(cp[:, 0, :], 0) + lanes_of(cp[:, 1, :], FD),
        lanes_of(sp[:, 0, :], 0) + lanes_of(sp[:, 1, :], TD),
    ]
    lines = jnp.concatenate(lines + [jnp.zeros((5, LANES), jnp.float32)], axis=0)
    ints[...] = (lines + 0.5).astype(jnp.int32)
    ints[3:4, :FD] = dest[...]
    ints[4:5, :FD] = part[...]
    loaded(0, 4)
    first_step(faces, f_col, f_row, f_first, f_send, FD)

    @pl.when((sec > 0) & (sec < NS - 1))
    def _():
        pl.semaphore_wait(barrier, T + 1)

    @pl.when((sec == 0) | (sec == NS - 1))
    def _():
        pl.semaphore_wait(barrier, T - 1 + (1 if NS > 1 else 0))

    sources = [lambda peer: ints, lambda peer: f_send.at[peer], lambda peer: c_send.at[peer],
               lambda peer: f_msg, lambda peer: c_msg, lambda peer: out_msg.at[peer]]
    landings = [ints_all, f_all, c_all, f_tot, c_tot, out_all]
    start(0, sources[0], landings[0])
    start(1, sources[1], landings[1])

    @pl.when(sec < NS - 1)
    def _():
        lower_copy().start()

    loaded(9, 13)
    first_step(coarse, c_col, c_row, c_first, c_send, TD)
    start(2, sources[2], landings[2])
    ints_all[me] = ints[...]
    f_all[me] = f_send[me]
    c_all[me] = c_send[me]

    loaded(13, len(loads))
    arrive(0, sources[0], landings[0])
    to_scalar = pltpu.make_async_copy(ints_all, ints_sm, local_sem)
    to_scalar.start()

    def tables_of(row, n, second, marks, a, cs, at):
        onehot = jnp.where(iota((n, LANES), 0) == row, 1.0, 0.0).astype(jnp.bfloat16)
        half = FD * PK
        width = 2 * n
        cs[pl.ds(at, FD)] = pick(onehot, second)[half:].reshape(FD, PK, width)
        for side in range(2):
            a[pl.ds(at, FD), side * PK : (side + 1) * PK, :] = pick(onehot, marks[side])[:half].reshape(FD, PK, -1)

    def peaks_from(j, _):
        rows = ints_all[j]
        tables_of(rows[0:1], f_row.shape[1], f_second[...], f_marks, f_a, f_cs, j * FD)
        tables_of(rows[1:2], c_row.shape[1], c_second[...], c_marks, c_a, c_cs, j * FD)
        return 0

    lax.fori_loop(0, T, peaks_from, 0, unroll=4)

    to_scalar.wait()

    def second_step(block, n, second, sr, si, groups):
        rows = n // 2 // T
        per = T // groups
        images = block.shape[1]
        for group in range(groups):
            x = block[group * per : (group + 1) * per].reshape(per * images * 2 * rows, n)
            both = mm(x, second[...]).reshape(per * images, 2 * rows, 2 * n)
            p, q = both[:, :rows], both[:, rows:]
            special = (iota((1, rows, 1), 1) == 0) & (me == 0)
            at = slice(group * per * images, (group + 1) * per * images)
            sr[at, :rows, :] = p[:, :, :n] - jnp.where(special, 0.0, q[:, :, n:])
            si[at, :rows, :] = -(p[:, :, n:] + jnp.where(special, 0.0, q[:, :, :n]))
            sr[at, rows:, :] = q[:, :8, :n]
            si[at, rows:, :] = -q[:, :8, n:]

    def weights(rows, n):
        at = iota((rows + 8, n), 0)
        main = jnp.where((at == 0) & (me == 0), 1.0, 2.0)
        extra = jnp.where((at == rows) & (me == 0), 1.0, 0.0)
        return jnp.where(at < rows, main, extra)

    def cross_all(n, sr, si, xr, xi, inv, sums, own_of, other_of, msg):
        w = weights(n // 2 // T, n)

        def one(p, _):
            own, other = own_of(p), other_of(p)
            vr, vi, inverse, size = cross(sr[own], si[own], sr[other], si[other])
            xr[p], xi[p], inv[p] = vr, vi, inverse
            sums[pl.ds(p, 1), :] = fold(jnp.sum(size * w, axis=0, keepdims=True))
            return 0

        lax.fori_loop(0, pairs, one, 0, unroll=8)
        total = jnp.sum(sums[...], axis=1, keepdims=True)
        msg[...] = jnp.broadcast_to(to_row(total, 0), msg.shape)

    def score_all(n, tot, it, xr, xi, inv, a, cs, part):
        row = jnp.sum(tot[...], axis=0)[0:1]
        limit = 1.0 / (row * (0.05 / (n * n)) + 1e-6)
        shape = (pairs, LANES)
        column = jnp.sum(jnp.where(iota(shape, 1) == iota(shape, 0), limit, 0.0), axis=1, keepdims=True)
        it[...] = jnp.broadcast_to(column, it.shape)

        def one(p, _):
            scale = jnp.minimum(inv[p], it[pl.ds(p, 1), :])
            unit = jnp.concatenate([xr[p] * scale, xi[p] * scale], axis=0).astype(jnp.bfloat16)
            got = mm(a[p].astype(jnp.bfloat16), unit)
            table = cs[p]
            part[p] = fold(got[:PK] * table[:, :n] - got[PK:] * table[:, n:])
            return 0

        lax.fori_loop(0, pairs, one, 0, unroll=16)

    NF, NC = f_row.shape[1], c_row.shape[1]
    arrive(1, sources[1], landings[1])
    second_step(f_all, NF, f_second, f_sr, f_si, 2)
    cross_all(
        NF, f_sr, f_si, f_xr, f_xi, f_in, f_sums, lambda p: p,
        lambda p: jnp.clip(ints_sm[p // FD, 3, p % FD] * FD + ints_sm[p // FD, 4, p % FD], 0, pairs - 1), f_msg,
    )
    start(3, sources[3], landings[3])
    f_tot[me] = f_msg[...]
    arrive(2, sources[2], landings[2])
    second_step(c_all, NC, c_second, c_sr, c_si, 2)
    cross_all(
        NC, c_sr, c_si, c_xr, c_xi, c_in, c_sums, lambda p: p // per_tile,
        lambda p: jnp.clip(ints_sm[p // FD, 3, p % FD] * TD + ints_sm[p // FD, 4, p % FD] // per_tile, 0, T * TD - 1), c_msg,
    )
    start(4, sources[4], landings[4])
    c_tot[me] = c_msg[...]
    arrive(3, sources[3], landings[3])
    score_all(NF, f_tot, f_it, f_xr, f_xi, f_in, f_a, f_cs, f_part)
    arrive(4, sources[4], landings[4])
    score_all(NC, c_tot, c_it, c_xr, c_xi, c_in, c_a, c_cs, c_part)

    def gather(j, _):
        def column(part):
            block = part[pl.ds(j * FD, FD)].reshape(FD * PK, LANES)
            return jnp.sum(block, axis=1, keepdims=True)

        row = to_row(column(c_part), 0) + to_row(column(f_part), FD * PK)
        out_msg[j] = jnp.broadcast_to(row, (8, LANES))
        return 0

    lax.fori_loop(0, T, gather, 0, unroll=8)
    start(5, sources[5], landings[5])
    out_all[me] = out_msg[me]

    @pl.when(sec > 0)
    def _():
        lower_copy().wait_recv()

    @pl.when(sec == 0)
    def _():
        low[...] = jnp.zeros_like(low)

    n = f_row.shape[1]
    rows_s = n // 2 + 8

    def spectrum_s(image):
        got = mm(s_first[...], windowed(image, f_col[...], f_row[...])).astype(jnp.bfloat16)
        both = mm(got, f_second[...])
        p, q = both[:rows_s], both[rows_s:]
        return p[:, :n] - q[:, n:], -(p[:, n:] + q[:, :n])

    onehot = jnp.where(iota((n, LANES), 0) == ints[2:3], 1.0, 0.0).astype(jnp.bfloat16)
    cs_s = pick(onehot, f_second[...])[TD * PK : 2 * TD * PK]
    a_s = [pick(onehot, s_marks[side])[: TD * PK] for side in range(2)]
    columns = []
    for which in range(TD):
        ar, ai = spectrum_s(upper[which])
        br, bi = spectrum_s(low[which])
        xr, xi, inverse, size = cross(ar, ai, br, bi)
        total = jnp.sum(jnp.sum(size * s_weight[...], axis=0, keepdims=True), axis=1, keepdims=True)
        scale = jnp.minimum(inverse, 1.0 / (total * (0.05 / (n * n)) + 1e-6))
        unit = jnp.concatenate([xr * scale, xi * scale], axis=0).astype(jnp.bfloat16)
        at = slice(which * PK, (which + 1) * PK)
        fr = mm(a_s[0][at].astype(jnp.bfloat16), unit)
        fi = mm(a_s[1][at].astype(jnp.bfloat16), unit)
        columns.append(jnp.sum(fr * cs_s[at, :n] - fi * cs_s[at, n:], axis=1, keepdims=True))
    row = to_row(jnp.concatenate(columns, axis=0), 0)
    section_out[...] = to_grid(jnp.broadcast_to(row, (8, LANES)), 0, PK)[:TD] * (1.0 / n)

    for kind in range(5):
        sent(kind, sources[kind], landings[kind])

    @pl.when(sec < NS - 1)
    def _():
        lower_copy().wait_send()

    arrive(5, sources[5], landings[5])
    total = jnp.sum(out_all[...], axis=0)
    coarse_out[...] = to_grid(total, 0, PK) * (1.0 / NC)
    fine_out[...] = to_grid(total, FD, PK) * (1.0 / NF)
    sent(5, sources[5], landings[5])


def split_body(
    T, NS, intersection_faces, destination, partner, face_peaks, coarse, coarse_peaks,
    upper_faces, lower_faces, section_peaks,
):
    FD, TD, PK = intersection_faces.shape[0], coarse.shape[0], face_peaks.shape[2]
    NF, NC = intersection_faces.shape[-1], coarse.shape[-1]
    pairs = T * FD

    operands = [
        destination.reshape(1, FD), partner.reshape(1, FD), face_peaks, coarse_peaks, section_peaks,
        intersection_faces.reshape(FD, NF, NF), coarse,
        upper_faces.reshape(TD, NF, NF), lower_faces.reshape(TD, NF, NF),
    ] + [jnp.asarray(t) for t in (
        hann(NF) + hann(NC) + split_tables(NF, T) + split_tables(NC, T) + whole_tables(NF)
    )]
    fr, cr = NF // 2 // T + 8, NC // 2 // T + 8
    f32 = jnp.float32
    V = pltpu.VMEM
    kept = [(x.shape[1:] if x.ndim == 4 else x.shape, x.dtype) for x in operands]
    scratch = [V(*one) for index, one in enumerate(kept) if index != 8] + [
        pltpu.SemaphoreType.DMA((len(operands) - 1,)), V((8, LANES), jnp.int32),
        V((T, 8, LANES), jnp.int32), pltpu.SMEM((T, 8, LANES), jnp.int32),
        V((TD, NF, NF), jnp.bfloat16),
        V((T, FD, NF // T, NF), jnp.bfloat16), V((T, FD, NF // T, NF), jnp.bfloat16),
        V((T, TD, NC // T, NC), jnp.bfloat16), V((T, TD, NC // T, NC), jnp.bfloat16),
        V((pairs, fr, NF), f32), V((pairs, fr, NF), f32),
        V((T * TD, cr, NC), f32), V((T * TD, cr, NC), f32),
    ] + [V((pairs, fr, NF), f32)] * 3 + [V((pairs, cr, NC), f32)] * 3 + [
        V((pairs, 2 * PK, 2 * fr), f32), V((pairs, PK, 2 * NF), f32),
        V((pairs, 2 * PK, 2 * cr), f32), V((pairs, PK, 2 * NC), f32),
        V((pairs, LANES), f32), V((pairs, LANES), f32),
        V((8, LANES), f32), V((8, LANES), f32),
        V((T, 8, LANES), f32), V((T, 8, LANES), f32),
        V((pairs, NF), f32), V((pairs, NC), f32),
        V((pairs, PK, LANES), f32), V((pairs, PK, LANES), f32),
        V((T, 8, LANES), f32), V((T, 8, LANES), f32),
        pltpu.SemaphoreType.DMA((6, T)), pltpu.SemaphoreType.DMA((6, T)),
        pltpu.SemaphoreType.DMA((2,)), pltpu.SemaphoreType.DMA,
    ]
    fine, coarse_scores, section = pl.pallas_call(
        functools.partial(kernel, T, NS),
        out_shape=(
            jax.ShapeDtypeStruct((FD, PK), f32), jax.ShapeDtypeStruct((FD, PK), f32),
            jax.ShapeDtypeStruct((TD, PK), f32),
        ),
        in_specs=[pl.BlockSpec(memory_space=pltpu.HBM)] * len(operands),
        out_specs=(pl.BlockSpec(memory_space=pltpu.VMEM),) * 3,
        scratch_shapes=scratch,
        compiler_params=pltpu.CompilerParams(
            collective_id=0, has_side_effects=True, vmem_limit_bytes=60 * 1024 * 1024
        ),
    )(*operands)
    return fine.reshape(FD, 1, PK), coarse_scores, section.reshape(TD, 1, PK)


def choose(T, NS, *args):
    faces, coarse, peaks = args[0], args[4], args[3]
    fits = (
        faces.shape[1] == 1
        and peaks.shape[2] == 8
        and faces.shape[0] == 8
        and faces.shape[-1] // 2 % (8 * T) == 0
        and coarse.shape[-1] // 2 % (8 * T) == 0
        and T * faces.shape[0] <= LANES
    )
    return split_body(T, NS, *args) if fits else body(*args)


def solution(mesh):
    return jax.shard_map(
        functools.partial(choose, mesh.shape["tile"], mesh.shape["sec"]),
        mesh=mesh,
        in_specs=(
            P(("sec", "tile"), None, None, None),
            P(("sec", "tile"), None),
            P(("sec", "tile")),
            P(("sec", "tile"), None, None),
            P(("sec", "tile"), None, None),
            P(("sec", "tile"), None, None),
            P(("sec", "tile"), None, None, None),
            P(("sec", "tile"), None, None, None),
            P(("sec", "tile"), None, None),
        ),
        out_specs=(
            P(("sec", "tile"), None, None),
            P(("sec", "tile"), None),
            P(("sec", "tile"), None, None),
        ),
        check_vma=False,
    )
```
